512 devices in a mesh: section: 16 (over z_hi, y, core), seq: 32 (over z_lo, x).
Axes of the slice: x: 4, y: 4, z: 16 (z_hi: 2, z_lo: 8; z = z_hi * 8 + z_lo), core: 2. Of those that a mesh axis runs over, the one named last changes fastest.
Arguments:
- starting_carries: bfloat16 [32, 16, 128, 1024], P('seq', 'section'), may hold values from -9 to 9
- incoming_micro_loads: bfloat16 [2, 32, 2, 128, 1024], P(None, 'seq', None, None, 'section'), may hold values from -9 to 9
- layer_scaling_factor: float32 [16, 512], P('section'), may hold values from 0.1 to 1.9
- asking_matrix: bfloat16 [16, 512, 1024], P('section')
- lookup_matrix: bfloat16 [16, 512, 1024], P('section')
- content_matrix: bfloat16 [16, 512, 1024], P('section'), may hold values from -0.1875 to 0.1875
- emitting_matrix: bfloat16 [16, 512, 1024], P('section'), may hold values from -0.5 to 0.5
- rotation_turning: float32 [16, 5, 512], P('section'), may hold values from -1 to 1
- rotation_scaling: float32 [16, 5, 2, 512], P('section'), may hold values from 0.5 to 1.5
- higher_mate_lines: int32 [8, 5, 128], replicated, may hold values from 0 to 127, each once within a row
- piece_visibility_table: int32 [32, 2, 3], P('seq'), may hold values from 0 to 1, as said below
Outputs:
- emitted: bfloat16 [32, 16, 128, 1024], P('seq', 'section')
The draws below stay inside these ranges and needn't reach their ends.
Inputs may be any that keep to these rules, and one draw needn't show every extreme that they name: `higher_mate_lines`: each row lists every number of 0 .. 127 once. `piece_visibility_table`: entry [j, 0, 2] is 1 for every j.
All inputs are finite; a program needn't handle non-finite values.
Results may differ from the reference program's by a relative error of at most 0.04.
Values may be sent and summed in bfloat16 or wider, within the bound.
A program may use at most 128 MiB of HBM per device.

```python
import math
import jax
import jax.numpy as jnp
from jax import lax

FEATURE_COUNT = 1024
HEADS = 16
HDIM = 64
PIECE_LENGTH = 128
WIN = 3
MIXES = 5
TICKS = 3
CASCADE_PARTS = 8
SLOTS = 16
NBLK = 64
MICRO_LOAD_SIZE = 8192
HD = 1024
N_SEQ = 32


def key_matrix(key):
    return jax.random.normal(jax.random.fold_in(key, 11), (CASCADE_PARTS, 2, FEATURE_COUNT // 2, HD), jnp.float32) / math.sqrt(FEATURE_COUNT)


def draw_lookup_matrix(key, part):
    return key_matrix(key).reshape(SLOTS, FEATURE_COUNT // 2, HD).astype(jnp.bfloat16)


def draw_asking_matrix(key, part):
    own = jax.random.normal(jax.random.fold_in(key, 12), (CASCADE_PARTS, 2, FEATURE_COUNT // 2, HD), jnp.float32) / math.sqrt(FEATURE_COUNT)
    return own.reshape(SLOTS, FEATURE_COUNT // 2, HD).astype(jnp.bfloat16)


def field_values(key, count):
    values = jax.random.truncated_normal(jax.random.fold_in(key, 1), -4.0, 4.0, (count, MICRO_LOAD_SIZE // 2, 2, FEATURE_COUNT), jnp.float32)
    row_low = 0.1
    row_high = 1.0
    row_scale = jnp.exp(jax.random.uniform(jax.random.fold_in(key, 4), (count, MICRO_LOAD_SIZE // 2, 1, 1), jnp.float32, math.log(row_low), math.log(row_high)))
    column_scale = jnp.exp(jax.random.uniform(jax.random.fold_in(key, 5), (1, 1, 1, FEATURE_COUNT), jnp.float32, math.log(0.5), math.log(2.0)))
    return (values * row_scale * column_scale).reshape(count, MICRO_LOAD_SIZE, FEATURE_COUNT)


def draw_starting_carries(key, part):
    cascade_carries = field_values(jax.random.fold_in(key, 21), CASCADE_PARTS)
    cascade_carries = cascade_carries.reshape(CASCADE_PARTS, N_SEQ, 2, PIECE_LENGTH, FEATURE_COUNT).transpose(1, 0, 2, 3, 4)
    return cascade_carries.reshape(N_SEQ, SLOTS, PIECE_LENGTH, FEATURE_COUNT).astype(jnp.bfloat16)


def draw_incoming_micro_loads(key, part):
    batches = field_values(jax.random.fold_in(key, 22), TICKS - 1)
    return batches.reshape(TICKS - 1, N_SEQ, 2, PIECE_LENGTH, FEATURE_COUNT).astype(jnp.bfloat16)


def draw_piece_visibility_table(key, part):
    table = jax.random.randint(jax.random.fold_in(key, 31), (N_SEQ, 2, WIN), 0, 2, jnp.int32)
    return table.at[:, 0, WIN - 1].set(1)


def level_of(own_key, dims, pieces, smallest, top_value):
    loudness, own = 1.0, jax.random.fold_in(own_key, 6)
    for position, parts in pieces:
        heights = jnp.exp(jax.random.uniform(jax.random.fold_in(own, position), (parts,), jnp.float32, smallest / len(pieces), top_value / len(pieces)))
        loudness = loudness * jnp.repeat(heights, dims[position] // parts).reshape([-1 if axis == position else 1 for axis in range(len(dims))])
    return loudness


def noise(stream_key, shape, deviation, most, shards=(), held_as=jnp.bfloat16):
    values = deviation * jax.random.normal(stream_key, shape, jnp.float32)
    if shards:
        values = values * level_of(stream_key, shape, shards, -0.22, 0.18)
    return jnp.clip(values, -most, most).astype(held_as)


def setup_inputs(seed: int = 0) -> dict:
    key_of = jax.random.split(jax.random.key(seed), 12)
    starting_carries = draw_starting_carries(jax.random.fold_in(key_of[11], 71), 0)
    incoming_micro_loads = draw_incoming_micro_loads(jax.random.fold_in(key_of[11], 71), 0)
    layer_scaling_factor = jnp.clip(1.0 + 0.18 * jax.random.normal(key_of[2], (SLOTS, FEATURE_COUNT // 2), jnp.float32), 0.1, 1.9)
    asking_matrix = draw_asking_matrix(jax.random.fold_in(key_of[11], 71), 0)
    lookup_matrix = draw_lookup_matrix(jax.random.fold_in(key_of[11], 71), 0)
    content_matrix = noise(key_of[5], (SLOTS, FEATURE_COUNT // 2, HD), FEATURE_COUNT ** -0.5, 0.1875, ((0, 16),))
    emitting_matrix = noise(key_of[6], (SLOTS, HD // 2, FEATURE_COUNT), (HD // 8) ** -0.5, 0.5, ((0, 16),))
    rotation_turning = jnp.clip(jax.random.uniform(key_of[7], (SLOTS, MIXES, FEATURE_COUNT // 2), jnp.float32, -1.0, 1.0) * level_of(key_of[7], (SLOTS, MIXES, FEATURE_COUNT // 2), ((0, 16),), -0.4, 0.0), -1.0, 1.0)
    rotation_scaling = jnp.clip(1.0 + 0.1 * jax.random.normal(key_of[8], (SLOTS, MIXES, 2, FEATURE_COUNT // 2), jnp.float32), 0.5, 1.5)
    higher_mate_lines = jax.vmap(lambda own: jax.random.permutation(own, PIECE_LENGTH))(jax.random.split(key_of[9], CASCADE_PARTS * MIXES)).reshape((CASCADE_PARTS, MIXES, PIECE_LENGTH)).astype(jnp.int32)
    piece_visibility_table = draw_piece_visibility_table(jax.random.fold_in(key_of[11], 71), 0)
    return dict(starting_carries=starting_carries, incoming_micro_loads=incoming_micro_loads, layer_scaling_factor=layer_scaling_factor, asking_matrix=asking_matrix, lookup_matrix=lookup_matrix, content_matrix=content_matrix, emitting_matrix=emitting_matrix, rotation_turning=rotation_turning, rotation_scaling=rotation_scaling, higher_mate_lines=higher_mate_lines, piece_visibility_table=piece_visibility_table)


def attend_block(query_block, keys_pad, values_pad, mask_row, block_num):
    keys_here = lax.dynamic_slice_in_dim(keys_pad, block_num, WIN + 1, 0).reshape((WIN + 1) * PIECE_LENGTH, HEADS, HDIM)
    values_here = lax.dynamic_slice_in_dim(values_pad, block_num, WIN + 1, 0).reshape((WIN + 1) * PIECE_LENGTH, HEADS, HDIM)
    scores = jnp.einsum('qhd,khd->hqk', query_block.astype(jnp.float32), keys_here.astype(jnp.float32)) * 0.125
    block_flags = []
    for place in range(WIN):
        reach = WIN - place
        block_flags.append(jnp.logical_and(block_num - reach >= 0, mask_row[reach - 1] == 1))
    earlier_ok = jnp.repeat(jnp.stack(block_flags), PIECE_LENGTH)
    earlier_ok = jnp.broadcast_to(earlier_ok[None, :], (PIECE_LENGTH, WIN * PIECE_LENGTH))
    rows_pos = jnp.arange(PIECE_LENGTH, dtype=jnp.int32)
    causal = rows_pos[None, :] <= rows_pos[:, None]
    allowed = jnp.concatenate([earlier_ok, causal], axis=1)
    scores = jnp.where(allowed[None], scores, jnp.float32(-1e+30))
    top_score = lax.optimization_barrier(jnp.max(scores, axis=-1, keepdims=True))
    expo = jnp.exp(scores - top_score)
    probs = (expo / lax.optimization_barrier(jnp.sum(expo, axis=-1, keepdims=True))).astype(jnp.bfloat16)
    attended = jnp.einsum('hqk,khd->qhd', probs.astype(jnp.float32), values_here.astype(jnp.float32))
    return attended.astype(jnp.bfloat16)

def section_apply(cascade_carry, gain, query_w, key_w, value_w, out_w, angles, gains, pairing, piece_visibility_table):
    wide = cascade_carry.astype(jnp.float32)
    square_mean = lax.optimization_barrier(jnp.mean(wide * wide, axis=-1, keepdims=True))
    normed = (wide * lax.rsqrt(square_mean + 1e-06) * gain).astype(jnp.bfloat16)
    queries = jnp.dot(normed, query_w, preferred_element_type=jnp.float32).astype(jnp.bfloat16)
    keys_all = jnp.dot(normed, key_w, preferred_element_type=jnp.float32).astype(jnp.bfloat16)
    values_all = jnp.dot(normed, value_w, preferred_element_type=jnp.float32).astype(jnp.bfloat16)
    shape_blocks = (NBLK, PIECE_LENGTH, HEADS, HDIM)
    padding = jnp.zeros((WIN, PIECE_LENGTH, HEADS, HDIM), jnp.bfloat16)
    keys_pad = jnp.concatenate([padding, keys_all.reshape(shape_blocks)], axis=0)
    values_pad = jnp.concatenate([padding, values_all.reshape(shape_blocks)], axis=0)
    block_ids = jnp.arange(NBLK, dtype=jnp.int32)

    def one_block(items):
        return attend_block(items[0], keys_pad, values_pad, items[1], items[2])
    attended = lax.map(one_block, (queries.reshape(shape_blocks), piece_visibility_table, block_ids))
    attended = attended.reshape(MICRO_LOAD_SIZE, HD)
    mixed = (wide + jnp.dot(attended, out_w, preferred_element_type=jnp.float32)).astype(jnp.bfloat16)
    levels = NBLK.bit_length() - 1
    for layer in range(MIXES):
        span = 1 << layer % levels
        grouped = mixed.reshape(NBLK // (2 * span), 2, span, PIECE_LENGTH, FEATURE_COUNT).astype(jnp.float32)
        lower = grouped[:, 0]
        upper = grouped[:, 1]
        ordering = pairing[layer]
        inverse = jnp.argsort(ordering).astype(jnp.int32)
        cosine = jnp.cos(angles[layer])
        sine_part = jnp.sin(angles[layer])
        new_lower = gains[layer, 0] * (cosine * lower + sine_part * upper[:, :, ordering])
        new_upper = gains[layer, 1] * (cosine * upper - sine_part * lower[:, :, inverse])
        mixed = jnp.stack([new_lower, new_upper], axis=1).reshape(MICRO_LOAD_SIZE, FEATURE_COUNT).astype(jnp.bfloat16)
    return mixed

def reference(starting_carries, incoming_micro_loads, layer_scaling_factor, asking_matrix, lookup_matrix, content_matrix, emitting_matrix, rotation_turning, rotation_scaling, higher_mate_lines, piece_visibility_table):
    cascade_carries = starting_carries.reshape(N_SEQ, CASCADE_PARTS, 2, PIECE_LENGTH, FEATURE_COUNT).transpose(1, 0, 2, 3, 4).reshape(CASCADE_PARTS, MICRO_LOAD_SIZE, FEATURE_COUNT)
    fresh_all = incoming_micro_loads.reshape(TICKS - 1, MICRO_LOAD_SIZE, FEATURE_COUNT)
    gain_full = layer_scaling_factor.reshape(CASCADE_PARTS, FEATURE_COUNT)
    query_full = asking_matrix.reshape(CASCADE_PARTS, FEATURE_COUNT, HD)
    key_full = lookup_matrix.reshape(CASCADE_PARTS, FEATURE_COUNT, HD)
    value_full = content_matrix.reshape(CASCADE_PARTS, FEATURE_COUNT, HD)
    out_full = emitting_matrix.reshape(CASCADE_PARTS, HD, FEATURE_COUNT)
    angle_full = rotation_turning.reshape(CASCADE_PARTS, 2, MIXES, FEATURE_COUNT // 2).transpose(0, 2, 1, 3).reshape(CASCADE_PARTS, MIXES, FEATURE_COUNT)
    mixgain_full = rotation_scaling.reshape(CASCADE_PARTS, 2, MIXES, 2, FEATURE_COUNT // 2).transpose(0, 2, 3, 1, 4).reshape(CASCADE_PARTS, MIXES, 2, FEATURE_COUNT)
    mask_full = piece_visibility_table.reshape(NBLK, WIN)
    entering = cascade_carries
    leaving = cascade_carries
    for step_tick in range(TICKS):
        if step_tick > 0:
            entering = jnp.concatenate([fresh_all[step_tick - 1][None], leaving[:-1]], axis=0)

        def one_section(items):
            return section_apply(items[0], items[1], items[2], items[3], items[4], items[5], items[6], items[7], items[8], mask_full)
        leaving = lax.map(one_section, (entering, gain_full, query_full, key_full, value_full, out_full, angle_full, mixgain_full, higher_mate_lines))
    return leaving.reshape(CASCADE_PARTS, N_SEQ, 2, PIECE_LENGTH, FEATURE_COUNT).transpose(1, 0, 2, 3, 4).reshape(N_SEQ, SLOTS, PIECE_LENGTH, FEATURE_COUNT)
```

```python
import jax
import jax.numpy as jnp
from jax import lax
from jax.experimental import pallas as pl
from jax.experimental.pallas import tpu as pltpu
from jax.sharding import PartitionSpec as P

HEADS = 16
WIN = 3
MIXES = 5
TICKS = 3
ROWS = 128
CHUNK = 128
CHUNKS = 8
WIDE = 1024
HALO_PARTS = 2
PER_PART = CHUNKS // HALO_PARTS
BF = jnp.bfloat16
F32 = jnp.float32


def remote(src, dst, send_sem, recv_sem, section, seq):
    return pltpu.make_async_remote_copy(
        src_ref=src,
        dst_ref=dst,
        send_sem=send_sem,
        recv_sem=recv_sem,
        device_id={"section": section, "seq": seq},
        device_id_type=pl.DeviceIdType.MESH,
    )


def kernel(
    start_ref, fresh_ref, gain_ref, wq_ref, wk_ref, wv_ref, wo_ref, angle_ref, scale_ref,
    pairing_ref, table_ref,
    out_ref,
    weights, gains, angles, scales, entering, halo, normed, queries, keys, values, attended,
    mixed, row_in, row_out, col_in, col_out, onehot, coef, bias, fresh_in, fresh_full,
    weight_local, weight_send, weight_recv, param_local, param_send, param_recv,
    fresh_send, fresh_recv, full_send,
    halo_send, halo_recv, row_send, row_recv, col_send, col_recv, back_send, back_recv,
):
    slot = lax.axis_index("section")
    seq = lax.axis_index("seq")
    section = slot // 2
    half = slot % 2
    sister = slot + 1 - 2 * half
    x = seq % 4
    z = seq // 4
    zrow = z % 4
    zbase = z - zrow
    mine = 2 * x + half
    held = (zrow + x) % 4

    weight_refs = (wk_ref, wv_ref, wq_ref, wo_ref)
    place = pl.ds(pl.multiple_of(half * 512, 512), 512)
    local_weights = [
        pltpu.make_async_copy(ref.at[0], weights.at[k, place], weight_local.at[k])
        for k, ref in enumerate(weight_refs)
    ]
    param_pairs = (
        (gain_ref, gains.at[half]),
        (angle_ref.at[0], angles.at[half]),
        (scale_ref.at[0], scales.at[half]),
    )
    local_params = [
        pltpu.make_async_copy(src, dst, param_local.at[k]) for k, (src, dst) in enumerate(param_pairs)
    ]
    for copy in local_weights + local_params:
        copy.start()

    @pl.when(seq < 2)
    def _():
        halo[...] = jnp.zeros_like(halo)

    barrier = pltpu.get_barrier_semaphore()

    def greet(to_section, to_seq):
        pl.semaphore_signal(
            barrier, inc=1, device_id={"section": to_section, "seq": to_seq},
            device_id_type=pl.DeviceIdType.MESH,
        )

    for k in range(1, CHUNKS):
        peer = (mine + k) % CHUNKS
        greet(2 * section + peer % 2, 4 * z + peer // 2)
    for k in range(1, 4):
        greet(slot, 4 * (zbase + (zrow + k) % 4) + x)
    for k in range(CHUNKS):
        source = (mine + k) % CHUNKS
        source_seq = 4 * (zbase + (x - source // 2 + 4) % 4) + source // 2

        @pl.when(section > 0)
        def _():
            greet(2 * section - 2 + source % 2, source_seq)

        if k == 0:
            @pl.when(zrow > 0)
            def _():
                greet(2 * section + source % 2, source_seq)
        else:
            greet(2 * section + source % 2, source_seq)

    @pl.when(seq > 0)
    def _():
        greet(slot, seq - 1)

    has_extra = jnp.logical_or(half == 1, seq >= 2)
    gives_extra = jnp.logical_or(half == 0, seq < 30)

    @pl.when(has_extra)
    def _():
        greet(sister, seq - 2 * (1 - half))

    @pl.when(section == 0)
    def _():
        for k in range(1, 8):
            greet(2 * k + half, seq)

    for f in range(CHUNKS):
        entering[0, f] = start_ref[0, 0, :, f * CHUNK:(f + 1) * CHUNK]

    one = jnp.int32(1)
    zero = jnp.int32(0)
    expected = (
        7 + 3 + jnp.where(section < 7, 8 * one, zero) + 8 - jnp.where(zrow == 0, one, zero)
        + jnp.where(seq < 31, one, zero) + jnp.where(gives_extra, one, zero)
        + jnp.where(section > 0, one, zero)
    )
    pl.semaphore_wait(barrier, expected)

    def near_copy(t, part):
        span = pl.ds(part * PER_PART, PER_PART)
        return remote(
            entering.at[t, span], halo.at[t, half, span], halo_send.at[0, part],
            halo_recv.at[t, 0, part], slot, seq + 1,
        )

    def forward_copy(t, part):
        span = pl.ds(part * PER_PART, PER_PART)
        return remote(
            halo.at[t, half, span], halo.at[t, half, span], halo_send.at[1, part],
            halo_recv.at[t, 1, part], sister, seq,
        )

    def forward_wait(t, part):
        span = pl.ds(part * PER_PART, PER_PART)
        return remote(
            halo.at[t, 1 - half, span], halo.at[t, 1 - half, span], halo_send.at[1, part],
            halo_recv.at[t, 1, part], sister, seq,
        )

    def extra_copy(t, part):
        span = pl.ds(part * PER_PART, PER_PART)
        return remote(
            entering.at[t, span], halo.at[t, 2, span], halo_send.at[2, part],
            halo_recv.at[t, 2, part], sister, seq + 2 * half,
        )

    def near_wait(t, part):
        span = pl.ds(part * PER_PART, PER_PART)
        return remote(
            entering.at[t, span], halo.at[t, half, span], halo_send.at[0, part],
            halo_recv.at[t, 0, part], slot, seq,
        )

    def send_halo(t, part):
        @pl.when(seq < 31)
        def _():
            near_copy(t, part).start()

        @pl.when(gives_extra)
        def _():
            extra_copy(t, part).start()

    param_copies = [
        remote(src, dst, param_send.at[k], param_recv.at[k], sister, seq)
        for k, (src, dst) in enumerate(param_pairs)
    ]
    weight_copies = [
        remote(ref.at[0], weights.at[k, place], weight_send.at[k], weight_recv.at[k], sister, seq)
        for k, ref in enumerate(weight_refs)
    ]
    other = pl.ds(pl.multiple_of((1 - half) * 512, 512), 512)
    fresh_copy = remote(
        fresh_ref.at[:, 0, 1 - half], fresh_in, fresh_send, fresh_recv, sister, seq
    )
    for copy in param_copies:
        copy.start()
    for part in range(HALO_PARTS):
        send_halo(0, part)
    for copy in weight_copies:
        copy.start()
    fresh_copy.start()

    row_num = lax.broadcasted_iota(jnp.int32, (ROWS, ROWS), 0)
    col_num = lax.broadcasted_iota(jnp.int32, (ROWS, ROWS), 1)
    pairing = pairing_ref[section]
    for layer in range(MIXES):
        back = jnp.where(row_num == pairing[layer:layer + 1, :], F32(1), F32(0))
        onehot[layer, 0] = back.T.astype(BF)
        onehot[layer, 1] = back.astype(BF)

    drop = jnp.full((ROWS, ROWS), -1e30, F32)
    keep = jnp.zeros((ROWS, ROWS), F32)
    for place_num, reach in ((0, 2 + half), (1, 1 + half), (2, 3 - 2 * half)):
        seen = table_ref[0, half, reach - 1]
        inside = jnp.where(2 * seq + half - reach >= 0, one, zero)
        shown = jnp.full((ROWS, ROWS), seen * inside, jnp.int32)
        flags = jnp.where(shown == 1, keep, drop)
        bias[0:ROWS, place_num * ROWS:(place_num + 1) * ROWS] = flags
        bias[ROWS:2 * ROWS, place_num * ROWS:(place_num + 1) * ROWS] = flags
    causal = jnp.where(col_num <= row_num, keep, drop)
    bias[0:ROWS, 3 * ROWS:] = causal
    bias[ROWS:2 * ROWS, 3 * ROWS:] = causal

    for copy in local_params:
        copy.wait()
    for k, (_, dst) in enumerate(
        ((None, gains.at[1 - half]), (None, angles.at[1 - half]), (None, scales.at[1 - half]))
    ):
        remote(dst, dst, param_send.at[k], param_recv.at[k], sister, seq).wait_recv()
    feature_half = mine // 4
    features = pl.ds(pl.multiple_of((mine % 4) * CHUNK, CHUNK), CHUNK)
    angle = angles[feature_half, :, features]
    cosine = jnp.cos(angle)
    sine = jnp.sin(angle)
    for layer in range(MIXES):
        scale = scales[feature_half, layer, :, features]
        c = cosine[layer:layer + 1]
        n = sine[layer:layer + 1]
        coef[layer, 0:1] = scale[0:1] * c
        coef[layer, 1:2] = scale[0:1] * n
        coef[layer, 2:3] = scale[1:2] * c
        coef[layer, 3:4] = scale[1:2] * n

    def norm(block, place_num):
        total = jnp.zeros((ROWS, 1), F32)
        for f in range(CHUNKS):
            wide = block[f].astype(F32)
            total = total + jnp.sum(wide * wide, axis=-1, keepdims=True)
        factor = lax.rsqrt(total * (1.0 / WIDE) + 1e-6)
        for f in range(CHUNKS):
            part = pl.ds((f % 4) * CHUNK, CHUNK)
            gain = gains[f // 4, :, part]
            normed[place_num * ROWS:(place_num + 1) * ROWS, f * CHUNK:(f + 1) * CHUNK] = (
                block[f].astype(F32) * factor * gain
            ).astype(BF)

    def project(which, rows, target, scale=None):
        def one_part(k, carry):
            cols = pl.ds(pl.multiple_of(k * 256, 256), 256)
            product = jnp.dot(
                normed[rows, :], weights[which, :, cols], preferred_element_type=F32
            )
            if scale is None:
                target[rows, cols] = product.astype(BF)
            else:
                target[:, cols] = (product * scale).astype(BF)
            return carry

        lax.fori_loop(0, 4, one_part, 0)

    def await_weight(t, which):
        @pl.when(t == 0)
        def _():
            local_weights[which].wait()
            remote(
                weights.at[which, other], weights.at[which, other], weight_send.at[which],
                weight_recv.at[which], sister, seq,
            ).wait_recv()

    def mix(layer, lower, upper):
        count = len(lower)
        low = jnp.concatenate(lower, axis=1)
        up = jnp.concatenate(upper, axis=1)
        rows = [
            jnp.concatenate([coef[layer, k:k + 1]] * count, axis=1) for k in range(4)
        ]
        to_low = jnp.dot(onehot[layer, 0], up, preferred_element_type=F32)
        to_up = jnp.dot(onehot[layer, 1], low, preferred_element_type=F32)
        new_low = (rows[0] * low.astype(F32) + rows[1] * to_low).astype(BF)
        new_up = (rows[2] * up.astype(F32) - rows[3] * to_up).astype(BF)
        cut = lambda whole: [whole[:, k * CHUNK:(k + 1) * CHUNK] for k in range(count)]
        return cut(new_low), cut(new_up)

    def mix_all(layer, bit, blocks):
        lows = [b for b in range(len(blocks)) if not b >> bit & 1]
        ups = [b | 1 << bit for b in lows]
        new_low, new_up = mix(layer, [blocks[b] for b in lows], [blocks[b] for b in ups])
        result = list(blocks)
        for k, b in enumerate(lows):
            result[b] = new_low[k]
        for k, b in enumerate(ups):
            result[b] = new_up[k]
        return result

    lane = lax.broadcasted_iota(jnp.int32, (1, CHUNK), 1)
    first_head = jnp.where(lane < 64, F32(1), F32(0))
    pick_first = first_head.astype(BF)
    pick_second = (1 - first_head).astype(BF)

    def tick(t, carry):
        for part in range(HALO_PARTS):
            @pl.when(t > 0)
            def _():
                for f in range(part * PER_PART, (part + 1) * PER_PART):
                    piece = remote(
                        entering.at[t, f], entering.at[t, f], back_send.at[0],
                        back_recv.at[t, f], slot, seq,
                    )
                    if f == 0:
                        @pl.when(section > 0)
                        def _():
                            piece.wait_recv()
                    else:
                        piece.wait_recv()
                send_halo(t, part)

        norm(entering.at[t], 3)
        own_rows = pl.ds(3 * ROWS, ROWS)
        await_weight(t, 0)
        project(0, own_rows, keys)
        await_weight(t, 1)
        project(1, own_rows, values)
        await_weight(t, 2)
        project(2, own_rows, queries, scale=0.125)

        @pl.when(t == 0)
        def _():
            fresh_copy.wait_recv()
            for k in range(TICKS - 1):
                own = fresh_ref[k, 0, half].astype(F32)
                theirs = fresh_in[k].astype(F32)
                even = jnp.concatenate([own, theirs], axis=1)
                odd = jnp.concatenate([theirs, own], axis=1)
                fresh_full[k] = jnp.where(half == 0, even, odd).astype(BF)

                @pl.when(section == 0)
                def _():
                    entering[k + 1, 0] = fresh_full[k]

                @pl.when(section > 0)
                def _():
                    remote(
                        fresh_full.at[k], entering.at[k + 1, section], full_send.at[k],
                        back_recv.at[k + 1, section], half, seq,
                    ).start()

        for part in range(HALO_PARTS):
            @pl.when(seq > 0)
            def _():
                near_wait(t, part).wait_recv()
                forward_copy(t, part).start()
        for part in range(HALO_PARTS):
            @pl.when(has_extra)
            def _():
                extra_copy(t, part).wait_recv()
        norm(halo.at[t, 2], 2)
        for part in range(HALO_PARTS):
            @pl.when(seq > 0)
            def _():
                forward_wait(t, part).wait_recv()
        norm(halo.at[t, 0], 0)
        norm(halo.at[t, 1], 1)
        near_rows = pl.ds(0, 3 * ROWS)
        project(0, near_rows, keys)
        project(1, near_rows, values)

        def two_heads(k, carry):
            cols = pl.ds(pl.multiple_of(k * CHUNK, CHUNK), CHUNK)
            both = queries[:, cols]
            stacked = jnp.concatenate([both * pick_first, both * pick_second], axis=0)
            scores = lax.dot_general(
                stacked, keys[:, cols], (((1,), (1,)), ((), ())), preferred_element_type=F32
            ) + bias[...]
            top = jnp.max(scores, axis=-1, keepdims=True)
            expo = jnp.exp(scores - top)
            total = jnp.sum(expo, axis=-1, keepdims=True)
            summed = jnp.dot(expo.astype(BF), values[:, cols], preferred_element_type=F32) / total
            attended[:, cols] = jnp.where(lane < 64, summed[:ROWS], summed[ROWS:]).astype(BF)
            return carry

        lax.fori_loop(0, CHUNKS, two_heads, 0)
        await_weight(t, 3)

        sends = []
        for away in (2, 1, 3, 0):
            target = (x + away) % 4
            cols = pl.ds(pl.multiple_of(target * 256, 256), 256)
            product = jnp.dot(attended[...], weights[3, :, cols], preferred_element_type=F32)
            for c in range(2):
                f = 2 * target + c
                mixed[f] = (
                    entering[t, f].astype(F32) + product[:, c * CHUNK:(c + 1) * CHUNK]
                ).astype(BF)
            if away:
                for c in range(2):
                    copy = remote(
                        mixed.at[2 * target + c], row_in.at[t, mine],
                        row_send.at[2 * away - 1 + c], row_recv.at[t, mine],
                        2 * section + c, 4 * z + target,
                    )
                    copy.start()
                    sends.append(copy)
            else:
                copy = remote(
                    mixed.at[2 * x + 1 - half], row_in.at[t, mine], row_send.at[0],
                    row_recv.at[t, mine], sister, seq,
                )
                copy.start()
                sends.append(copy)
        row_in[t, mine] = mixed[mine]
        for k in range(1, CHUNKS):
            source = (mine + k) % CHUNKS
            remote(
                row_in.at[t, source], row_in.at[t, source], row_send.at[0],
                row_recv.at[t, source], slot, seq,
            ).wait_recv()
        blocks = [row_in[t, b] for b in range(CHUNKS)]
        for layer in range(3):
            blocks = mix_all(layer, layer, blocks)
        for b in range(CHUNKS):
            row_out[b] = blocks[b]

        for k in (2, 1, 3):
            target = (zrow + k) % 4
            pair = (target + x) % 4
            copy = remote(
                row_out.at[pl.ds(2 * pair, 2)], col_in.at[t, zrow], col_send.at[k - 1],
                col_recv.at[t, zrow], slot, 4 * (zbase + target) + x,
            )
            copy.start()
            sends.append(copy)
        for c in range(2):
            col_in[t, zrow, c] = row_out[2 * held + c]
        for k in range(1, 4):
            source = (zrow + k) % 4
            remote(
                col_in.at[t, source], col_in.at[t, source], col_send.at[0],
                col_recv.at[t, source], slot, seq,
            ).wait_recv()
        blocks = [col_in[t, r, c] for r in range(4) for c in range(2)]
        for layer in range(3, MIXES):
            blocks = mix_all(layer, layer - 2, blocks)
        for b in range(CHUNKS):
            col_out[b] = blocks[b]

        ahead = jnp.where(t < TICKS - 1, one, zero)
        for k in range(4):
            target = (zrow + k) % 4
            for m in range(2):
                c = (half + m) % 2

                def back_copy():
                    return remote(
                        col_out.at[2 * target + c], entering.at[t + 1, mine],
                        back_send.at[2 * k + m], back_recv.at[t + 1, mine],
                        2 * (section + ahead) + c, 4 * (zbase + target) + held,
                    )

                if k == 0 and m == 0:
                    itself = jnp.logical_and(t == TICKS - 1, zrow == 0)

                    @pl.when(itself)
                    def _():
                        entering[t + 1, mine] = col_out[2 * target + c]

                    @pl.when(jnp.logical_and(
                        jnp.logical_not(itself), jnp.logical_or(t == TICKS - 1, section < 7)
                    ))
                    def _():
                        back_copy().start()
                else:
                    @pl.when(jnp.logical_or(t == TICKS - 1, section < 7))
                    def _():
                        back_copy().start()

        for copy in sends:
            copy.wait_send()
        for part in range(HALO_PARTS):
            @pl.when(seq < 31)
            def _():
                near_copy(t, part).wait_send()

            @pl.when(gives_extra)
            def _():
                extra_copy(t, part).wait_send()

            @pl.when(seq > 0)
            def _():
                forward_copy(t, part).wait_send()

        @pl.when(jnp.logical_or(t == TICKS - 1, section < 7))
        def _():
            for k in range(4):
                for m in range(2):
                    target = (zrow + k) % 4
                    c = (half + m) % 2
                    sent = remote(
                        col_out.at[2 * target + c], entering.at[t + 1, mine],
                        back_send.at[2 * k + m], back_recv.at[t + 1, mine],
                        slot, seq,
                    )
                    if k or m:
                        sent.wait_send()
                    else:
                        @pl.when(jnp.logical_or(t < TICKS - 1, zrow > 0))
                        def _():
                            sent.wait_send()

        @pl.when(t == 0)
        def _():
            for copy in param_copies + weight_copies + [fresh_copy]:
                copy.wait_send()

            @pl.when(section > 0)
            def _():
                for k in range(TICKS - 1):
                    remote(
                        fresh_full.at[k], entering.at[k + 1, section], full_send.at[k],
                        back_recv.at[k + 1, section], half, seq,
                    ).wait_send()

        return carry

    lax.fori_loop(0, TICKS, tick, 0)

    for f in range(CHUNKS):
        piece = remote(
            entering.at[TICKS, f], entering.at[TICKS, f], back_send.at[0],
            back_recv.at[TICKS, f], slot, seq,
        )

        @pl.when(jnp.logical_or(zrow > 0, mine != f))
        def _():
            piece.wait_recv()

        out_ref[0, 0, :, f * CHUNK:(f + 1) * CHUNK] = entering[TICKS, f]


def local(*args):
    dma = pltpu.SemaphoreType.DMA
    vmem = pl.BlockSpec(memory_space=pltpu.VMEM)
    hbm = pl.BlockSpec(memory_space=pl.ANY)
    smem = pl.BlockSpec(memory_space=pltpu.SMEM)
    block = (CHUNKS, ROWS, CHUNK)
    return pl.pallas_call(
        kernel,
        out_shape=jax.ShapeDtypeStruct((1, 1, ROWS, WIDE), BF),
        in_specs=[vmem, vmem, vmem, hbm, hbm, hbm, hbm, vmem, vmem, vmem, smem],
        out_specs=vmem,
        scratch_shapes=[
            pltpu.VMEM((4, WIDE, WIDE), BF),
            pltpu.VMEM((2, 1, 512), F32),
            pltpu.VMEM((2, MIXES, 512), F32),
            pltpu.VMEM((2, MIXES, 2, 512), F32),
            pltpu.VMEM((TICKS + 1,) + block, BF),
            pltpu.VMEM((TICKS, 3) + block, BF),
            pltpu.VMEM((4 * ROWS, WIDE), BF),
            pltpu.VMEM((ROWS, WIDE), BF),
            pltpu.VMEM((4 * ROWS, WIDE), BF),
            pltpu.VMEM((4 * ROWS, WIDE), BF),
            pltpu.VMEM((ROWS, WIDE), BF),
            pltpu.VMEM(block, BF),
            pltpu.VMEM((TICKS,) + block, BF),
            pltpu.VMEM(block, BF),
            pltpu.VMEM((TICKS, 4, 2, ROWS, CHUNK), BF),
            pltpu.VMEM(block, BF),
            pltpu.VMEM((MIXES, 2, ROWS, ROWS), BF),
            pltpu.VMEM((MIXES, 4, CHUNK), F32),
            pltpu.VMEM((2 * ROWS, 4 * ROWS), F32),
            pltpu.VMEM((TICKS - 1, ROWS, 64), BF),
            pltpu.VMEM((TICKS - 1, ROWS, CHUNK), BF),
            dma((4,)), dma((4,)), dma((4,)), dma((3,)), dma((3,)), dma((3,)),
            dma, dma, dma((TICKS - 1,)),
            dma((3, HALO_PARTS)), dma((TICKS, 3, HALO_PARTS)),
            dma((7,)), dma((TICKS, CHUNKS)),
            dma((3,)), dma((TICKS, 4)),
            dma((CHUNKS,)), dma((TICKS + 1, CHUNKS)),
        ],
        compiler_params=pltpu.CompilerParams(
            collective_id=0, has_side_effects=True, vmem_limit_bytes=48 * 1024 * 1024
        ),
    )(*args)


def solution(mesh):
    in_specs = (
        P("seq", "section", None, None),
        P(None, "seq", None, None, "section"),
        P("section", None),
        P("section", None, None),
        P("section", None, None),
        P("section", None, None),
        P("section", None, None),
        P("section", None, None),
        P("section", None, None, None),
        P(),
        P("seq", None, None),
    )
    out_specs = P("seq", "section", None, None)

    def run(start, fresh, gain, asking, lookup, content, emitting, turning, scaling, lines, table):
        return jax.shard_map(
            local, mesh=mesh, in_specs=in_specs, out_specs=out_specs, check_vma=False
        )(start, fresh, gain, asking, lookup, content, emitting, turning, scaling, lines, table)

    return run
```

```python
import jax
import jax.numpy as jnp
from jax import lax
from jax.experimental import pallas as pl
from jax.experimental.pallas import tpu as pltpu
from jax.sharding import PartitionSpec as P

HEADS = 16
WIN = 3
MIXES = 5
TICKS = 3
FAR = 4
ROWS = 128
CHUNK = 128
CHUNKS = 8
WIDE = 1024
HALO_PARTS = 2
PER_PART = CHUNKS // HALO_PARTS
BF = jnp.bfloat16
F32 = jnp.float32


def remote(src, dst, send_sem, recv_sem, section, seq):
    return pltpu.make_async_remote_copy(
        src_ref=src,
        dst_ref=dst,
        send_sem=send_sem,
        recv_sem=recv_sem,
        device_id={"section": section, "seq": seq},
        device_id_type=pl.DeviceIdType.MESH,
    )


def kernel(
    start_ref, fresh_ref, gain_ref, wq_ref, wk_ref, wv_ref, wo_ref, angle_ref, scale_ref,
    pairing_ref, table_ref,
    out_ref,
    weights, gains, angles, scales, entering, halo, normed, queries, keys, values, attended,
    mixed, row_in, row_out, col_in, col_out, onehot, coef, bias, fresh_own, fresh_in, fresh_full,
    pairing, relay,
    start_sem, pairing_sem, fresh_sem, relay_send, relay_recv,
    weight_local, weight_send, weight_recv, param_local, param_send, param_recv,
    fresh_send, fresh_recv, full_send,
    halo_send, halo_recv, row_send, row_recv, col_send, col_recv, back_send, back_recv,
):
    slot = lax.axis_index("section")
    seq = lax.axis_index("seq")
    section = slot // 2
    half = slot % 2
    sister = slot + 1 - 2 * half
    x = seq % 4
    z = seq // 4
    zrow = z % 4
    zbase = z - zrow
    mine = 2 * x + half
    held = (zrow + x) % 4

    weight_refs = (wk_ref, wv_ref, wq_ref, wo_ref)
    place = pl.ds(pl.multiple_of(half * 512, 512), 512)
    local_weights = [
        pltpu.make_async_copy(ref.at[0], weights.at[k, place], weight_local.at[k])
        for k, ref in enumerate(weight_refs)
    ]
    param_pairs = (
        (gain_ref, gains.at[half]),
        (angle_ref, angles.at[half]),
        (scale_ref.at[0], scales.at[half]),
    )
    local_params = [
        pltpu.make_async_copy(src, dst, param_local.at[k]) for k, (src, dst) in enumerate(param_pairs)
    ]
    local_starts = [
        pltpu.make_async_copy(
            start_ref.at[0, 0, :, pl.ds(f * CHUNK, CHUNK)], entering.at[0, f], start_sem.at[f]
        )
        for f in range(CHUNKS)
    ]
    local_pairing = pltpu.make_async_copy(pairing_ref, pairing, pairing_sem)
    local_fresh = pltpu.make_async_copy(fresh_ref.at[:, 0, half], fresh_own, fresh_sem)
    for copy in local_starts + local_params + [local_pairing] + local_weights + [local_fresh]:
        copy.start()

    @pl.when(seq < 2)
    def _():
        halo[...] = jnp.zeros_like(halo)

    barrier = pltpu.get_barrier_semaphore()

    def greet(to_section, to_seq):
        pl.semaphore_signal(
            barrier, inc=1, device_id={"section": to_section, "seq": to_seq},
            device_id_type=pl.DeviceIdType.MESH,
        )

    for k in range(1, CHUNKS):
        peer = (mine + k) % CHUNKS
        greet(2 * section + peer % 2, 4 * z + peer // 2)
    for k in range(1, 4):
        greet(slot, 4 * (zbase + (zrow + k) % 4) + x)
    for k in range(CHUNKS):
        source = (mine + k) % CHUNKS
        source_seq = 4 * (zbase + (x - source // 2 + 4) % 4) + source // 2

        @pl.when(jnp.logical_and(
            section > 0, jnp.logical_or(section != FAR, source // 2 == 3)
        ))
        def _():
            greet(2 * section - 2 + source % 2, source_seq)

        if k == 0:
            @pl.when(zrow > 0)
            def _():
                greet(2 * section + source % 2, source_seq)
        else:
            greet(2 * section + source % 2, source_seq)

    @pl.when(seq > 0)
    def _():
        greet(slot, seq - 1)

    has_extra = jnp.logical_or(half == 1, seq >= 2)
    gives_extra = jnp.logical_or(half == 0, seq < 30)

    @pl.when(has_extra)
    def _():
        greet(sister, seq - 2 * (1 - half))

    @pl.when(section == 0)
    def _():
        for k in range(1, 8):
            greet(2 * k + half, seq)

    relays = section < 3
    relay_seq = 4 * (zbase + (x - section + 8) % 4) + section % 4

    @pl.when(relays)
    def _():
        for c in range(2):
            greet(2 * (FAR - 1) + c, relay_seq)

    @pl.when(section == FAR)
    def _():
        for k in range(3):
            greet(2 * k + half, seq)

    for copy in local_starts:
        copy.wait()

    one = jnp.int32(1)
    zero = jnp.int32(0)
    expected = (
        7 + 3 + jnp.where(section < 7, 8 * one, zero) + 8 - jnp.where(zrow == 0, one, zero)
        + jnp.where(seq < 31, one, zero) + jnp.where(gives_extra, one, zero)
        + jnp.where(section > 0, one, zero) + jnp.where(relays, one, zero)
    )
    pl.semaphore_wait(barrier, expected)

    def near_copy(t, part):
        span = pl.ds(part * PER_PART, PER_PART)
        return remote(
            entering.at[t, span], halo.at[t, half, span], halo_send.at[0, part],
            halo_recv.at[t, 0, part], slot, seq + 1,
        )

    def forward_copy(t, part):
        span = pl.ds(part * PER_PART, PER_PART)
        return remote(
            halo.at[t, half, span], halo.at[t, half, span], halo_send.at[1, part],
            halo_recv.at[t, 1, part], sister, seq,
        )

    def forward_wait(t, part):
        span = pl.ds(part * PER_PART, PER_PART)
        return remote(
            halo.at[t, 1 - half, span], halo.at[t, 1 - half, span], halo_send.at[1, part],
            halo_recv.at[t, 1, part], sister, seq,
        )

    def extra_copy(t, part):
        span = pl.ds(part * PER_PART, PER_PART)
        return remote(
            entering.at[t, span], halo.at[t, 2, span], halo_send.at[2, part],
            halo_recv.at[t, 2, part], sister, seq + 2 * half,
        )

    def near_wait(t, part):
        span = pl.ds(part * PER_PART, PER_PART)
        return remote(
            entering.at[t, span], halo.at[t, half, span], halo_send.at[0, part],
            halo_recv.at[t, 0, part], slot, seq,
        )

    def send_halo(t, part):
        @pl.when(seq < 31)
        def _():
            near_copy(t, part).start()

        @pl.when(gives_extra)
        def _():
            extra_copy(t, part).start()

    param_copies = [
        remote(src, dst, param_send.at[k], param_recv.at[k], sister, seq)
        for k, (src, dst) in enumerate(param_pairs)
    ]
    weight_copies = [
        remote(ref.at[0], weights.at[k, place], weight_send.at[k], weight_recv.at[k], sister, seq)
        for k, ref in enumerate(weight_refs)
    ]
    other = pl.ds(pl.multiple_of((1 - half) * 512, 512), 512)
    fresh_copy = remote(
        fresh_ref.at[:, 0, 1 - half], fresh_in, fresh_send, fresh_recv, sister, seq
    )
    for copy in param_copies:
        copy.start()
    for part in range(HALO_PARTS):
        send_halo(0, part)
    for copy in weight_copies:
        copy.start()
    fresh_copy.start()

    row_num = lax.broadcasted_iota(jnp.int32, (ROWS, ROWS), 0)
    col_num = lax.broadcasted_iota(jnp.int32, (ROWS, ROWS), 1)
    local_pairing.wait()
    for layer in range(MIXES):
        lines = pairing[layer, pl.ds(section, 1), :]
        back = jnp.where(row_num == lines, F32(1), F32(0))
        onehot[layer, 0] = back.T.astype(BF)
        onehot[layer, 1] = back.astype(BF)

    drop = jnp.full((ROWS, ROWS), -1e30, F32)
    keep = jnp.zeros((ROWS, ROWS), F32)
    for place_num, reach in ((0, 2 + half), (1, 1 + half), (2, 3 - 2 * half)):
        seen = table_ref[0, half, reach - 1]
        inside = jnp.where(2 * seq + half - reach >= 0, one, zero)
        shown = jnp.full((ROWS, ROWS), seen * inside, jnp.int32)
        flags = jnp.where(shown == 1, keep, drop)
        bias[0:ROWS, place_num * ROWS:(place_num + 1) * ROWS] = flags
        bias[ROWS:2 * ROWS, place_num * ROWS:(place_num + 1) * ROWS] = flags
    causal = jnp.where(col_num <= row_num, keep, drop)
    bias[0:ROWS, 3 * ROWS:] = causal
    bias[ROWS:2 * ROWS, 3 * ROWS:] = causal

    for copy in local_params:
        copy.wait()
    for k, (_, dst) in enumerate(
        ((None, gains.at[1 - half]), (None, angles.at[1 - half]), (None, scales.at[1 - half]))
    ):
        remote(dst, dst, param_send.at[k], param_recv.at[k], sister, seq).wait_recv()
    feature_half = mine // 4
    features = pl.ds(pl.multiple_of((mine % 4) * CHUNK, CHUNK), CHUNK)
    angle = angles[feature_half, :, 0, features]
    cosine = jnp.cos(angle)
    sine = jnp.sin(angle)
    for layer in range(MIXES):
        scale = scales[feature_half, layer, :, features]
        c = cosine[layer:layer + 1]
        n = sine[layer:layer + 1]
        coef[layer, 0:1] = scale[0:1] * c
        coef[layer, 1:2] = scale[0:1] * n
        coef[layer, 2:3] = scale[1:2] * c
        coef[layer, 3:4] = scale[1:2] * n

    def norm(block, place_num):
        total = jnp.zeros((ROWS, 1), F32)
        for f in range(CHUNKS):
            wide = block[f].astype(F32)
            total = total + jnp.sum(wide * wide, axis=-1, keepdims=True)
        factor = lax.rsqrt(total * (1.0 / WIDE) + 1e-6)
        for f in range(CHUNKS):
            part = pl.ds((f % 4) * CHUNK, CHUNK)
            gain = gains[f // 4, :, part]
            normed[place_num * ROWS:(place_num + 1) * ROWS, f * CHUNK:(f + 1) * CHUNK] = (
                block[f].astype(F32) * factor * gain
            ).astype(BF)

    def project(which, rows, target, scale=None):
        def one_part(k, carry):
            cols = pl.ds(pl.multiple_of(k * 256, 256), 256)
            product = jnp.dot(
                normed[rows, :], weights[which, :, cols], preferred_element_type=F32
            )
            if scale is None:
                target[rows, cols] = product.astype(BF)
            else:
                target[:, cols] = (product * scale).astype(BF)
            return carry

        lax.fori_loop(0, 4, one_part, 0)

    def await_weight(t, which):
        @pl.when(t == 0)
        def _():
            local_weights[which].wait()
            remote(
                weights.at[which, other], weights.at[which, other], weight_send.at[which],
                weight_recv.at[which], sister, seq,
            ).wait_recv()

    def mix(layer, lower, upper):
        count = len(lower)
        low = jnp.concatenate(lower, axis=1)
        up = jnp.concatenate(upper, axis=1)
        rows = [
            jnp.concatenate([coef[layer, k:k + 1]] * count, axis=1) for k in range(4)
        ]
        to_low = jnp.dot(onehot[layer, 0], up, preferred_element_type=F32)
        to_up = jnp.dot(onehot[layer, 1], low, preferred_element_type=F32)
        new_low = (rows[0] * low.astype(F32) + rows[1] * to_low).astype(BF)
        new_up = (rows[2] * up.astype(F32) - rows[3] * to_up).astype(BF)
        cut = lambda whole: [whole[:, k * CHUNK:(k + 1) * CHUNK] for k in range(count)]
        return cut(new_low), cut(new_up)

    def mix_all(layer, bit, blocks):
        lows = [b for b in range(len(blocks)) if not b >> bit & 1]
        ups = [b | 1 << bit for b in lows]
        new_low, new_up = mix(layer, [blocks[b] for b in lows], [blocks[b] for b in ups])
        result = list(blocks)
        for k, b in enumerate(lows):
            result[b] = new_low[k]
        for k, b in enumerate(ups):
            result[b] = new_up[k]
        return result

    lane = lax.broadcasted_iota(jnp.int32, (1, CHUNK), 1)
    first_head = jnp.where(lane < 64, F32(1), F32(0))
    pick_first = first_head.astype(BF)
    pick_second = (1 - first_head).astype(BF)

    def tick(t, carry):
        for part in range(HALO_PARTS):
            @pl.when(t > 0)
            def _():
                for f in range(part * PER_PART, (part + 1) * PER_PART):
                    piece = remote(
                        entering.at[t, f], entering.at[t, f], back_send.at[0],
                        back_recv.at[t, f], slot, seq,
                    )
                    if f == 0:
                        @pl.when(section > 0)
                        def _():
                            piece.wait_recv()
                    else:
                        piece.wait_recv()
                send_halo(t, part)

        norm(entering.at[t], 3)
        own_rows = pl.ds(3 * ROWS, ROWS)
        await_weight(t, 0)
        project(0, own_rows, keys)
        await_weight(t, 1)
        project(1, own_rows, values)
        await_weight(t, 2)
        project(2, own_rows, queries, scale=0.125)

        @pl.when(t == 0)
        def _():
            local_fresh.wait()
            fresh_copy.wait_recv()
            for k in range(TICKS - 1):
                own = fresh_own[k].astype(F32)
                theirs = fresh_in[k].astype(F32)
                even = jnp.concatenate([own, theirs], axis=0)
                odd = jnp.concatenate([theirs, own], axis=0)
                fresh_full[k] = jnp.where(half == 0, even, odd).T.astype(BF)

                @pl.when(section == 0)
                def _():
                    entering[k + 1, 0] = fresh_full[k]

                @pl.when(section > 0)
                def _():
                    remote(
                        fresh_full.at[k], entering.at[k + 1, section], full_send.at[k],
                        back_recv.at[k + 1, section], half, seq,
                    ).start()

        for part in range(HALO_PARTS):
            @pl.when(seq > 0)
            def _():
                near_wait(t, part).wait_recv()
                forward_copy(t, part).start()
        for part in range(HALO_PARTS):
            @pl.when(has_extra)
            def _():
                extra_copy(t, part).wait_recv()
        norm(halo.at[t, 2], 2)
        for part in range(HALO_PARTS):
            @pl.when(seq > 0)
            def _():
                forward_wait(t, part).wait_recv()
        norm(halo.at[t, 0], 0)
        norm(halo.at[t, 1], 1)
        near_rows = pl.ds(0, 3 * ROWS)
        project(0, near_rows, keys)
        project(1, near_rows, values)

        def two_heads(k, carry):
            cols = pl.ds(pl.multiple_of(k * CHUNK, CHUNK), CHUNK)
            both = queries[:, cols]
            stacked = jnp.concatenate([both * pick_first, both * pick_second], axis=0)
            scores = lax.dot_general(
                stacked, keys[:, cols], (((1,), (1,)), ((), ())), preferred_element_type=F32
            ) + bias[...]
            top = jnp.max(scores, axis=-1, keepdims=True)
            expo = jnp.exp(scores - top)
            total = jnp.sum(expo, axis=-1, keepdims=True)
            summed = jnp.dot(expo.astype(BF), values[:, cols], preferred_element_type=F32) / total
            attended[:, cols] = jnp.where(lane < 64, summed[:ROWS], summed[ROWS:]).astype(BF)
            return carry

        lax.fori_loop(0, CHUNKS, two_heads, 0)
        await_weight(t, 3)

        sends = []
        for away in (2, 1, 3, 0):
            target = (x + away) % 4
            cols = pl.ds(pl.multiple_of(target * 256, 256), 256)
            product = jnp.dot(attended[...], weights[3, :, cols], preferred_element_type=F32)
            for c in range(2):
                f = 2 * target + c
                mixed[f] = (
                    entering[t, f].astype(F32) + product[:, c * CHUNK:(c + 1) * CHUNK]
                ).astype(BF)
            if away:
                for c in range(2):
                    copy = remote(
                        mixed.at[2 * target + c], row_in.at[t, mine],
                        row_send.at[2 * away - 1 + c], row_recv.at[t, mine],
                        2 * section + c, 4 * z + target,
                    )
                    copy.start()
                    sends.append(copy)
            else:
                copy = remote(
                    mixed.at[2 * x + 1 - half], row_in.at[t, mine], row_send.at[0],
                    row_recv.at[t, mine], sister, seq,
                )
                copy.start()
                sends.append(copy)
        row_in[t, mine] = mixed[mine]
        for k in range(1, CHUNKS):
            source = (mine + k) % CHUNKS
            remote(
                row_in.at[t, source], row_in.at[t, source], row_send.at[0],
                row_recv.at[t, source], slot, seq,
            ).wait_recv()
        blocks = [row_in[t, b] for b in range(CHUNKS)]
        for layer in range(3):
            blocks = mix_all(layer, layer, blocks)
        for b in range(CHUNKS):
            row_out[b] = blocks[b]

        for k in (2, 1, 3):
            target = (zrow + k) % 4
            pair = (target + x) % 4
            copy = remote(
                row_out.at[pl.ds(2 * pair, 2)], col_in.at[t, zrow], col_send.at[k - 1],
                col_recv.at[t, zrow], slot, 4 * (zbase + target) + x,
            )
            copy.start()
            sends.append(copy)
        for c in range(2):
            col_in[t, zrow, c] = row_out[2 * held + c]
        for k in range(1, 4):
            source = (zrow + k) % 4
            remote(
                col_in.at[t, source], col_in.at[t, source], col_send.at[0],
                col_recv.at[t, source], slot, seq,
            ).wait_recv()
        blocks = [col_in[t, r, c] for r in range(4) for c in range(2)]
        for layer in range(3, MIXES):
            blocks = mix_all(layer, layer - 2, blocks)
        for b in range(CHUNKS):
            col_out[b] = blocks[b]

        ahead = jnp.where(t < TICKS - 1, one, zero)
        last = t == TICKS - 1
        by_relay = jnp.logical_and(jnp.logical_and(section == FAR - 1, x < 3), t < TICKS - 1)
        direct = jnp.logical_and(
            jnp.logical_or(last, section < 7), jnp.logical_not(by_relay)
        )
        for k in range(4):
            target = (zrow + k) % 4
            for m in range(2):
                c = (half + m) % 2

                def back_copy():
                    return remote(
                        col_out.at[2 * target + c], entering.at[t + 1, mine],
                        back_send.at[2 * k + m], back_recv.at[t + 1, mine],
                        2 * (section + ahead) + c, 4 * (zbase + target) + held,
                    )

                if k == 0 and m == 0:
                    itself = jnp.logical_and(t == TICKS - 1, zrow == 0)

                    @pl.when(itself)
                    def _():
                        entering[t + 1, mine] = col_out[2 * target + c]

                    @pl.when(jnp.logical_and(jnp.logical_not(itself), direct))
                    def _():
                        back_copy().start()
                else:
                    @pl.when(direct)
                    def _():
                        back_copy().start()

                @pl.when(by_relay)
                def _():
                    remote(
                        col_out.at[2 * target + c], relay.at[t, half],
                        back_send.at[2 * k + m], relay_recv.at[t, half],
                        2 * x + c, 4 * (zbase + target) + held,
                    ).start()

        @pl.when(jnp.logical_and(relays, t < TICKS - 1))
        def _():
            for c in range(2):
                remote(
                    relay.at[t, c], relay.at[t, c], relay_send.at[c], relay_recv.at[t, c],
                    slot, seq,
                ).wait_recv()
                remote(
                    relay.at[t, c], entering.at[t + 1, 2 * section + c], relay_send.at[c],
                    back_recv.at[t + 1, 2 * section + c], 2 * FAR + half, seq,
                ).start()
            for c in range(2):
                remote(
                    relay.at[t, c], relay.at[t, c], relay_send.at[c], relay_recv.at[t, c],
                    slot, seq,
                ).wait_send()

        for copy in sends:
            copy.wait_send()
        for part in range(HALO_PARTS):
            @pl.when(seq < 31)
            def _():
                near_copy(t, part).wait_send()

            @pl.when(gives_extra)
            def _():
                extra_copy(t, part).wait_send()

            @pl.when(seq > 0)
            def _():
                forward_copy(t, part).wait_send()

        @pl.when(jnp.logical_or(t == TICKS - 1, section < 7))
        def _():
            for k in range(4):
                for m in range(2):
                    target = (zrow + k) % 4
                    c = (half + m) % 2
                    sent = remote(
                        col_out.at[2 * target + c], entering.at[t + 1, mine],
                        back_send.at[2 * k + m], back_recv.at[t + 1, mine],
                        slot, seq,
                    )
                    if k or m:
                        sent.wait_send()
                    else:
                        @pl.when(jnp.logical_or(t < TICKS - 1, zrow > 0))
                        def _():
                            sent.wait_send()

        @pl.when(t == 0)
        def _():
            for copy in param_copies + weight_copies + [fresh_copy]:
                copy.wait_send()

            @pl.when(section > 0)
            def _():
                for k in range(TICKS - 1):
                    remote(
                        fresh_full.at[k], entering.at[k + 1, section], full_send.at[k],
                        back_recv.at[k + 1, section], half, seq,
                    ).wait_send()

        return carry

    lax.fori_loop(0, TICKS, tick, 0)

    for f in range(CHUNKS):
        piece = remote(
            entering.at[TICKS, f], entering.at[TICKS, f], back_send.at[0],
            back_recv.at[TICKS, f], slot, seq,
        )

        @pl.when(jnp.logical_or(zrow > 0, mine != f))
        def _():
            piece.wait_recv()

        out_ref[0, 0, :, f * CHUNK:(f + 1) * CHUNK] = entering[TICKS, f]


def local(*args):
    dma = pltpu.SemaphoreType.DMA
    vmem = pl.BlockSpec(memory_space=pltpu.VMEM)
    hbm = pl.BlockSpec(memory_space=pltpu.HBM)
    smem = pl.BlockSpec(memory_space=pltpu.SMEM)
    block = (CHUNKS, ROWS, CHUNK)
    return pl.pallas_call(
        kernel,
        out_shape=jax.ShapeDtypeStruct((1, 1, ROWS, WIDE), BF),
        in_specs=[hbm] * 10 + [smem],
        out_specs=vmem,
        scratch_shapes=[
            pltpu.VMEM((4, WIDE, WIDE), BF),
            pltpu.VMEM((2, 1, 512), F32),
            pltpu.VMEM((2, MIXES, 1, 512), F32),
            pltpu.VMEM((2, MIXES, 2, 512), F32),
            pltpu.VMEM((TICKS + 1,) + block, BF),
            pltpu.VMEM((TICKS, 3) + block, BF),
            pltpu.VMEM((4 * ROWS, WIDE), BF),
            pltpu.VMEM((ROWS, WIDE), BF),
            pltpu.VMEM((4 * ROWS, WIDE), BF),
            pltpu.VMEM((4 * ROWS, WIDE), BF),
            pltpu.VMEM((ROWS, WIDE), BF),
            pltpu.VMEM(block, BF),
            pltpu.VMEM((TICKS,) + block, BF),
            pltpu.VMEM(block, BF),
            pltpu.VMEM((TICKS, 4, 2, ROWS, CHUNK), BF),
            pltpu.VMEM(block, BF),
            pltpu.VMEM((MIXES, 2, ROWS, ROWS), BF),
            pltpu.VMEM((MIXES, 4, CHUNK), F32),
            pltpu.VMEM((2 * ROWS, 4 * ROWS), F32),
            pltpu.VMEM((TICKS - 1, 64, ROWS), BF),
            pltpu.VMEM((TICKS - 1, 64, ROWS), BF),
            pltpu.VMEM((TICKS - 1, ROWS, CHUNK), BF),
            pltpu.VMEM((MIXES, 8, ROWS), jnp.int32),
            pltpu.VMEM((TICKS - 1, 2, ROWS, CHUNK), BF),
            dma((CHUNKS,)), dma, dma, dma((2,)), dma((TICKS - 1, 2)),
            dma((4,)), dma((4,)), dma((4,)), dma((3,)), dma((3,)), dma((3,)),
            dma, dma, dma((TICKS - 1,)),
            dma((3, HALO_PARTS)), dma((TICKS, 3, HALO_PARTS)),
            dma((7,)), dma((TICKS, CHUNKS)),
            dma((3,)), dma((TICKS, 4)),
            dma((CHUNKS,)), dma((TICKS + 1, CHUNKS)),
        ],
        compiler_params=pltpu.CompilerParams(
            collective_id=0, has_side_effects=True, vmem_limit_bytes=60 * 1024 * 1024
        ),
    )(*args)


def solution(mesh):
    in_specs = (
        P("seq", "section", None, None),
        P(None, "seq", None, "section", None),
        P("section", None),
        P("section", None, None),
        P("section", None, None),
        P("section", None, None),
        P("section", None, None),
        P(None, "section", None),
        P("section", None, None, None),
        P(),
        P("seq", None, None),
    )
    out_specs = P("seq", "section", None, None)

    def run(start, fresh, gain, asking, lookup, content, emitting, turning, scaling, lines, table):
        return jax.shard_map(
            local, mesh=mesh, in_specs=in_specs, out_specs=out_specs, check_vma=False
        )(
            start, jnp.swapaxes(fresh, 3, 4), gain, asking, lookup, content, emitting,
            jnp.swapaxes(turning, 0, 1), scaling, jnp.swapaxes(lines, 0, 1), table,
        )

    return run
```

```python
import jax
import jax.numpy as jnp
from jax import lax
from jax.experimental import pallas as pl
from jax.experimental.pallas import tpu as pltpu
from jax.sharding import PartitionSpec as P

HEADS = 16
WIN = 3
MIXES = 5
TICKS = 3
FAR = 4
ROWS = 128
CHUNK = 128
CHUNKS = 8
WIDE = 1024
HALO_PARTS = 4
PER_PART = CHUNKS // HALO_PARTS
BF = jnp.bfloat16
F32 = jnp.float32


def remote(src, dst, send_sem, recv_sem, section, seq):
    return pltpu.make_async_remote_copy(
        src_ref=src,
        dst_ref=dst,
        send_sem=send_sem,
        recv_sem=recv_sem,
        device_id={"section": section, "seq": seq},
        device_id_type=pl.DeviceIdType.MESH,
    )


def kernel(
    start_ref, fresh_ref, gain_ref, wq_ref, wk_ref, wv_ref, wo_ref, angle_ref, scale_ref,
    pairing_ref, table_ref,
    out_ref,
    weights, gains, angles, scales, entering, halo, normed, queries, keys, values, attended,
    mixed, row_in, row_out, col_in, col_out, onehot, coef, bias, fresh_own, fresh_in, fresh_full,
    pairing, relay,
    start_sem, pairing_sem, fresh_sem, relay_send, relay_recv,
    weight_local, weight_send, weight_recv, param_local, param_send, param_recv,
    fresh_send, fresh_recv, full_send,
    near_send, near_recv, ahead_send, halo_send, halo_recv, row_send, row_recv, col_send, col_recv, back_send, back_recv,
):
    slot = lax.axis_index("section")
    seq = lax.axis_index("seq")
    section = slot // 2
    half = slot % 2
    sister = slot + 1 - 2 * half
    x = seq % 4
    z = seq // 4
    zrow = z % 4
    zbase = z - zrow
    mine = 2 * x + half
    held = (zrow + x) % 4

    weight_refs = (wk_ref, wv_ref, wq_ref, wo_ref)
    place = pl.ds(pl.multiple_of(half * 512, 512), 512)
    local_weights = [
        pltpu.make_async_copy(ref.at[0], weights.at[k, place], weight_local.at[k])
        for k, ref in enumerate(weight_refs)
    ]
    param_pairs = (
        (gain_ref, gains.at[half]),
        (angle_ref, angles.at[half]),
        (scale_ref.at[0], scales.at[half]),
    )
    local_params = [
        pltpu.make_async_copy(src, dst, param_local.at[k]) for k, (src, dst) in enumerate(param_pairs)
    ]
    local_starts = [
        pltpu.make_async_copy(
            start_ref.at[0, 0, :, pl.ds(f * CHUNK, CHUNK)], entering.at[0, f], start_sem.at[f]
        )
        for f in range(CHUNKS)
    ]
    local_pairing = pltpu.make_async_copy(pairing_ref, pairing, pairing_sem)
    local_fresh = pltpu.make_async_copy(fresh_ref.at[:, 0, half], fresh_own, fresh_sem)
    for copy in local_starts + local_params + [local_pairing] + local_weights + [local_fresh]:
        copy.start()

    @pl.when(seq < 2)
    def _():
        halo[...] = jnp.zeros_like(halo)

    barrier = pltpu.get_barrier_semaphore()

    def greet(to_section, to_seq):
        pl.semaphore_signal(
            barrier, inc=1, device_id={"section": to_section, "seq": to_seq},
            device_id_type=pl.DeviceIdType.MESH,
        )

    for k in range(1, CHUNKS):
        peer = (mine + k) % CHUNKS
        greet(2 * section + peer % 2, 4 * z + peer // 2)
    for k in range(1, 4):
        greet(slot, 4 * (zbase + (zrow + k) % 4) + x)
    for k in range(CHUNKS):
        source = (mine + k) % CHUNKS
        source_seq = 4 * (zbase + (x - source // 2 + 4) % 4) + source // 2

        @pl.when(jnp.logical_and(
            section > 0, jnp.logical_or(section != FAR, source // 2 == 3)
        ))
        def _():
            greet(2 * section - 2 + source % 2, source_seq)

        if k == 0:
            @pl.when(zrow > 0)
            def _():
                greet(2 * section + source % 2, source_seq)
        else:
            greet(2 * section + source % 2, source_seq)

    @pl.when(seq > 0)
    def _():
        greet(slot, seq - 1)

    fed = jnp.logical_and(section != 0, section != FAR)
    feeds = jnp.logical_and(section != 7, section != FAR - 1)
    before = jnp.maximum(seq - 1, 0)

    @pl.when(jnp.logical_and(fed, seq > 0))
    def _():
        for f in range(CHUNKS):
            row = (before % 4 - f // 2 + 4) % 4
            greet(2 * section - 2 + f % 2, 4 * (before // 16 * 4 + row) + f // 2)

    has_extra = jnp.logical_or(half == 1, seq >= 2)
    gives_extra = jnp.logical_or(half == 0, seq < 30)

    @pl.when(has_extra)
    def _():
        greet(sister, seq - 2 * (1 - half))

    @pl.when(section == 0)
    def _():
        for k in range(1, 8):
            greet(2 * k + half, seq)

    relays = section < 3
    relay_seq = 4 * (zbase + (x - section + 8) % 4) + section % 4

    @pl.when(relays)
    def _():
        for c in range(2):
            greet(2 * (FAR - 1) + c, relay_seq)

    @pl.when(section == FAR)
    def _():
        for k in range(3):
            greet(2 * k + half, seq)

    for copy in local_starts:
        copy.wait()

    one = jnp.int32(1)
    zero = jnp.int32(0)
    expected = (
        7 + 3 + jnp.where(section < 7, 8 * one, zero) + 8 - jnp.where(zrow == 0, one, zero)
        + jnp.where(seq < 31, one, zero) + jnp.where(gives_extra, one, zero)
        + jnp.where(section > 0, one, zero) + jnp.where(relays, one, zero)
        + jnp.where(feeds, 8 * one, zero)
        - jnp.where(
            jnp.logical_and(feeds, jnp.logical_and(held == 3, zbase == 4)), 2 * one, zero
        )
    )
    pl.semaphore_wait(barrier, expected)

    def near_copy(t, f, to_seq):
        return remote(
            entering.at[t, f], halo.at[t, half, f], near_send.at[f], near_recv.at[t, f],
            slot, to_seq,
        )

    def by_neighbor(t):
        return jnp.logical_or(t == 0, jnp.logical_not(fed))

    def forward_copy(t, part):
        span = pl.ds(PER_PART * part, PER_PART)
        return remote(
            halo.at[t, half, span], halo.at[t, half, span], halo_send.at[1, part],
            halo_recv.at[t, 1, part], sister, seq,
        )

    def forward_wait(t, part):
        span = pl.ds(PER_PART * part, PER_PART)
        return remote(
            halo.at[t, 1 - half, span], halo.at[t, 1 - half, span], halo_send.at[1, part],
            halo_recv.at[t, 1, part], sister, seq,
        )

    def extra_copy(t, part):
        span = pl.ds(PER_PART * part, PER_PART)
        return remote(
            entering.at[t, span], halo.at[t, 2, span], halo_send.at[2, part],
            halo_recv.at[t, 2, part], sister, seq + 2 * half,
        )

    def relay_wait(t, c):
        return remote(
            relay.at[t, c], relay.at[t, c], relay_send.at[t, c], relay_recv.at[t, c], slot, seq
        )

    def send_halo(t, part):
        @pl.when(jnp.logical_and(seq < 31, by_neighbor(t)))
        def _():
            for c in range(PER_PART):
                near_copy(t, PER_PART * part + c, seq + 1).start()

        @pl.when(gives_extra)
        def _():
            extra_copy(t, part).start()

    param_copies = [
        remote(src, dst, param_send.at[k], param_recv.at[k], sister, seq)
        for k, (src, dst) in enumerate(param_pairs)
    ]
    weight_copies = [
        remote(ref.at[0], weights.at[k, place], weight_send.at[k], weight_recv.at[k], sister, seq)
        for k, ref in enumerate(weight_refs)
    ]
    other = pl.ds(pl.multiple_of((1 - half) * 512, 512), 512)
    fresh_copy = remote(
        fresh_ref.at[:, 0, 1 - half], fresh_in, fresh_send, fresh_recv, sister, seq
    )
    for copy in param_copies:
        copy.start()
    for part in range(HALO_PARTS):
        send_halo(0, part)
    for copy in weight_copies:
        copy.start()
    fresh_copy.start()

    row_num = lax.broadcasted_iota(jnp.int32, (ROWS, ROWS), 0)
    col_num = lax.broadcasted_iota(jnp.int32, (ROWS, ROWS), 1)
    local_pairing.wait()
    for layer in range(MIXES):
        lines = pairing[layer, pl.ds(section, 1), :]
        back = jnp.where(row_num == lines, F32(1), F32(0))
        onehot[layer, 0] = back.T.astype(BF)
        onehot[layer, 1] = back.astype(BF)

    drop = jnp.full((ROWS, ROWS), -1e30, F32)
    keep = jnp.zeros((ROWS, ROWS), F32)
    for place_num, reach in ((0, 2 + half), (1, 1 + half), (2, 3 - 2 * half)):
        seen = table_ref[0, half, reach - 1]
        inside = jnp.where(2 * seq + half - reach >= 0, one, zero)
        shown = jnp.full((ROWS, ROWS), seen * inside, jnp.int32)
        flags = jnp.where(shown == 1, keep, drop)
        bias[0:ROWS, place_num * ROWS:(place_num + 1) * ROWS] = flags
        bias[ROWS:2 * ROWS, place_num * ROWS:(place_num + 1) * ROWS] = flags
    causal = jnp.where(col_num <= row_num, keep, drop)
    bias[0:ROWS, 3 * ROWS:] = causal
    bias[ROWS:2 * ROWS, 3 * ROWS:] = causal

    for copy in local_params:
        copy.wait()
    for k, (_, dst) in enumerate(
        ((None, gains.at[1 - half]), (None, angles.at[1 - half]), (None, scales.at[1 - half]))
    ):
        remote(dst, dst, param_send.at[k], param_recv.at[k], sister, seq).wait_recv()
    feature_half = mine // 4
    features = pl.ds(pl.multiple_of((mine % 4) * CHUNK, CHUNK), CHUNK)
    angle = angles[feature_half, :, 0, features]
    cosine = jnp.cos(angle)
    sine = jnp.sin(angle)
    for layer in range(MIXES):
        scale = scales[feature_half, layer, :, features]
        c = cosine[layer:layer + 1]
        n = sine[layer:layer + 1]
        coef[layer, 0:1] = scale[0:1] * c
        coef[layer, 1:2] = scale[0:1] * n
        coef[layer, 2:3] = scale[1:2] * c
        coef[layer, 3:4] = scale[1:2] * n

    def norm(block, place_num):
        total = jnp.zeros((ROWS, 1), F32)
        for f in range(CHUNKS):
            wide = block[f].astype(F32)
            total = total + jnp.sum(wide * wide, axis=-1, keepdims=True)
        factor = lax.rsqrt(total * (1.0 / WIDE) + 1e-6)
        for f in range(CHUNKS):
            part = pl.ds((f % 4) * CHUNK, CHUNK)
            gain = gains[f // 4, :, part]
            normed[place_num * ROWS:(place_num + 1) * ROWS, f * CHUNK:(f + 1) * CHUNK] = (
                block[f].astype(F32) * factor * gain
            ).astype(BF)

    def project(which, rows, target, scale=None):
        def one_part(k, carry):
            cols = pl.ds(pl.multiple_of(k * 256, 256), 256)
            product = jnp.dot(
                normed[rows, :], weights[which, :, cols], preferred_element_type=F32
            )
            if scale is None:
                target[rows, cols] = product.astype(BF)
            else:
                target[:, cols] = (product * scale).astype(BF)
            return carry

        lax.fori_loop(0, 4, one_part, 0, unroll=4)

    def await_weight(t, which):
        @pl.when(t == 0)
        def _():
            local_weights[which].wait()
            remote(
                weights.at[which, other], weights.at[which, other], weight_send.at[which],
                weight_recv.at[which], sister, seq,
            ).wait_recv()

    def mix(layer, lower, upper):
        count = len(lower)
        low = jnp.concatenate(lower, axis=1)
        up = jnp.concatenate(upper, axis=1)
        rows = [
            jnp.concatenate([coef[layer, k:k + 1]] * count, axis=1) for k in range(4)
        ]
        to_low = jnp.dot(onehot[layer, 0], up, preferred_element_type=F32)
        to_up = jnp.dot(onehot[layer, 1], low, preferred_element_type=F32)
        new_low = (rows[0] * low.astype(F32) + rows[1] * to_low).astype(BF)
        new_up = (rows[2] * up.astype(F32) - rows[3] * to_up).astype(BF)
        cut = lambda whole: [whole[:, k * CHUNK:(k + 1) * CHUNK] for k in range(count)]
        return cut(new_low), cut(new_up)

    def mix_all(layer, bit, blocks):
        lows = [b for b in range(len(blocks)) if not b >> bit & 1]
        ups = [b | 1 << bit for b in lows]
        new_low, new_up = mix(layer, [blocks[b] for b in lows], [blocks[b] for b in ups])
        result = list(blocks)
        for k, b in enumerate(lows):
            result[b] = new_low[k]
        for k, b in enumerate(ups):
            result[b] = new_up[k]
        return result

    lane = lax.broadcasted_iota(jnp.int32, (1, CHUNK), 1)
    first_head = jnp.where(lane < 64, F32(1), F32(0))
    pick_first = first_head.astype(BF)
    pick_second = (1 - first_head).astype(BF)

    def ahead_copy(t, k, m):
        target = (zrow + k) % 4
        c = (half + m) % 2
        pair = 4 * (zbase + target) + held
        return pair, remote(
            col_out.at[2 * target + c], halo.at[t + 1, c, mine], ahead_send.at[2 * k + m],
            near_recv.at[t + 1, mine], 2 * section + 2 + c, jnp.minimum(pair + 1, 31),
        )

    def back_sent(t):
        @pl.when(jnp.logical_or(t == TICKS - 1, section < 7))
        def _():
            for k in range(4):
                for m in range(2):
                    target = (zrow + k) % 4
                    c = (half + m) % 2
                    sent = remote(
                        col_out.at[2 * target + c], entering.at[t + 1, mine],
                        back_send.at[2 * k + m], back_recv.at[t + 1, mine],
                        slot, seq,
                    )
                    if k or m:
                        sent.wait_send()
                    else:
                        @pl.when(jnp.logical_or(t < TICKS - 1, zrow > 0))
                        def _():
                            sent.wait_send()

        @pl.when(jnp.logical_and(feeds, t < TICKS - 1))
        def _():
            for k in range(4):
                for m in range(2):
                    pair, copy_ahead = ahead_copy(t, k, m)

                    @pl.when(pair < 31)
                    def _():
                        copy_ahead.wait_send()

    def tick(t, carry):
        for step in range(HALO_PARTS):
            part = (x - zrow + step + 4) % 4

            @pl.when(t > 0)
            def _():
                for c in range(PER_PART):
                    f = PER_PART * part + c
                    piece = remote(
                        entering.at[t, f], entering.at[t, f], back_send.at[0],
                        back_recv.at[t, f], slot, seq,
                    )
                    if c == 0:
                        @pl.when(jnp.logical_or(section > 0, part > 0))
                        def _():
                            piece.wait_recv()
                    else:
                        piece.wait_recv()
                send_halo(t, part)

        norm(entering.at[t], 3)
        own_rows = pl.ds(3 * ROWS, ROWS)
        await_weight(t, 0)
        project(0, own_rows, keys)
        await_weight(t, 1)
        project(1, own_rows, values)
        await_weight(t, 2)
        project(2, own_rows, queries, scale=0.125)

        @pl.when(t == 0)
        def _():
            local_fresh.wait()
            fresh_copy.wait_recv()
            for k in range(TICKS - 1):
                own = fresh_own[k].astype(F32)
                theirs = fresh_in[k].astype(F32)
                even = jnp.concatenate([own, theirs], axis=0)
                odd = jnp.concatenate([theirs, own], axis=0)
                fresh_full[k] = jnp.where(half == 0, even, odd).T.astype(BF)

                @pl.when(section == 0)
                def _():
                    entering[k + 1, 0] = fresh_full[k]

                @pl.when(section > 0)
                def _():
                    remote(
                        fresh_full.at[k], entering.at[k + 1, section], full_send.at[k],
                        back_recv.at[k + 1, section], half, seq,
                    ).start()

        for step in range(HALO_PARTS):
            part = (before % 4 - before // 4 % 4 + step + 4) % 4

            @pl.when(seq > 0)
            def _():
                for c in range(PER_PART):
                    near_copy(t, PER_PART * part + c, seq).wait_recv()
                forward_copy(t, part).start()
        for part in range(HALO_PARTS):
            @pl.when(has_extra)
            def _():
                extra_copy(t, part).wait_recv()
        norm(halo.at[t, 2], 2)
        for part in range(HALO_PARTS):
            @pl.when(seq > 0)
            def _():
                forward_wait(t, part).wait_recv()
        norm(halo.at[t, 0], 0)
        norm(halo.at[t, 1], 1)
        near_rows = pl.ds(0, 3 * ROWS)
        project(0, near_rows, keys)
        project(1, near_rows, values)

        def two_heads(k, carry):
            cols = pl.ds(pl.multiple_of(k * CHUNK, CHUNK), CHUNK)
            both = queries[:, cols]
            stacked = jnp.concatenate([both * pick_first, both * pick_second], axis=0)
            scores = lax.dot_general(
                stacked, keys[:, cols], (((1,), (1,)), ((), ())), preferred_element_type=F32
            ) + bias[...]
            top = jnp.max(scores, axis=-1, keepdims=True)
            expo = jnp.exp(scores - top)
            total = jnp.sum(expo, axis=-1, keepdims=True)
            summed = jnp.dot(expo.astype(BF), values[:, cols], preferred_element_type=F32) / total
            attended[:, cols] = jnp.where(lane < 64, summed[:ROWS], summed[ROWS:]).astype(BF)
            return carry

        lax.fori_loop(0, CHUNKS, two_heads, 0, unroll=4)
        await_weight(t, 3)

        @pl.when(t > 0)
        def _():
            back_sent(t - 1)

        sends = []
        for away in (2, 1, 3, 0):
            target = (x + away) % 4
            cols = pl.ds(pl.multiple_of(target * 256, 256), 256)
            product = jnp.dot(attended[...], weights[3, :, cols], preferred_element_type=F32)
            for c in range(2):
                f = 2 * target + c
                mixed[f] = (
                    entering[t, f].astype(F32) + product[:, c * CHUNK:(c + 1) * CHUNK]
                ).astype(BF)
            if away:
                for c in range(2):
                    copy = remote(
                        mixed.at[2 * target + c], row_in.at[t, mine],
                        row_send.at[2 * away - 1 + c], row_recv.at[t, mine],
                        2 * section + c, 4 * z + target,
                    )
                    copy.start()
                    sends.append(copy)
            else:
                copy = remote(
                    mixed.at[2 * x + 1 - half], row_in.at[t, mine], row_send.at[0],
                    row_recv.at[t, mine], sister, seq,
                )
                copy.start()
                sends.append(copy)
        row_in[t, mine] = mixed[mine]
        for k in range(1, CHUNKS):
            source = (mine + k) % CHUNKS
            remote(
                row_in.at[t, source], row_in.at[t, source], row_send.at[0],
                row_recv.at[t, source], slot, seq,
            ).wait_recv()
        blocks = [row_in[t, b] for b in range(CHUNKS)]
        for layer in range(3):
            blocks = mix_all(layer, layer, blocks)
        for b in range(CHUNKS):
            row_out[b] = blocks[b]

        for k in (2, 1, 3):
            target = (zrow + k) % 4
            pair = (target + x) % 4
            copy = remote(
                row_out.at[pl.ds(2 * pair, 2)], col_in.at[t, zrow], col_send.at[k - 1],
                col_recv.at[t, zrow], slot, 4 * (zbase + target) + x,
            )
            copy.start()
            sends.append(copy)
        for c in range(2):
            col_in[t, zrow, c] = row_out[2 * held + c]
        for k in range(1, 4):
            source = (zrow + k) % 4
            remote(
                col_in.at[t, source], col_in.at[t, source], col_send.at[0],
                col_recv.at[t, source], slot, seq,
            ).wait_recv()
        blocks = [col_in[t, r, c] for r in range(4) for c in range(2)]
        for layer in range(3, MIXES):
            blocks = mix_all(layer, layer - 2, blocks)
        for b in range(CHUNKS):
            col_out[b] = blocks[b]

        ahead = jnp.where(t < TICKS - 1, one, zero)
        last = t == TICKS - 1
        by_relay = jnp.logical_and(jnp.logical_and(section == FAR - 1, x < 3), t < TICKS - 1)
        direct = jnp.logical_and(
            jnp.logical_or(last, section < 7), jnp.logical_not(by_relay)
        )
        for k in range(4):
            target = (zrow + k) % 4
            for m in range(2):
                c = (half + m) % 2

                def back_copy():
                    return remote(
                        col_out.at[2 * target + c], entering.at[t + 1, mine],
                        back_send.at[2 * k + m], back_recv.at[t + 1, mine],
                        2 * (section + ahead) + c, 4 * (zbase + target) + held,
                    )

                if k == 0 and m == 0:
                    itself = jnp.logical_and(t == TICKS - 1, zrow == 0)

                    @pl.when(itself)
                    def _():
                        entering[t + 1, mine] = col_out[2 * target + c]

                    @pl.when(jnp.logical_and(jnp.logical_not(itself), direct))
                    def _():
                        back_copy().start()
                else:
                    @pl.when(direct)
                    def _():
                        back_copy().start()

                @pl.when(by_relay)
                def _():
                    remote(
                        col_out.at[2 * target + c], relay.at[t, half],
                        back_send.at[2 * k + m], relay_recv.at[t, half],
                        2 * x + c, 4 * (zbase + target) + held,
                    ).start()

        @pl.when(jnp.logical_and(feeds, t < TICKS - 1))
        def _():
            for k in range(4):
                for m in range(2):
                    pair, copy_ahead = ahead_copy(t, k, m)

                    @pl.when(pair < 31)
                    def _():
                        copy_ahead.start()

        @pl.when(jnp.logical_and(relays, t < TICKS - 1))
        def _():
            for c in range(2):
                relay_wait(t, c).wait_recv()
                remote(
                    relay.at[t, c], entering.at[t + 1, 2 * section + c], relay_send.at[t, c],
                    back_recv.at[t + 1, 2 * section + c], 2 * FAR + half, seq,
                ).start()

        for copy in sends:
            copy.wait_send()
        for part in range(HALO_PARTS):
            @pl.when(jnp.logical_and(seq < 31, by_neighbor(t)))
            def _():
                for c in range(PER_PART):
                    near_copy(t, PER_PART * part + c, seq + 1).wait_send()

            @pl.when(gives_extra)
            def _():
                extra_copy(t, part).wait_send()

            @pl.when(seq > 0)
            def _():
                forward_copy(t, part).wait_send()

        @pl.when(t == 0)
        def _():
            for copy in param_copies + weight_copies + [fresh_copy]:
                copy.wait_send()

            @pl.when(section > 0)
            def _():
                for k in range(TICKS - 1):
                    remote(
                        fresh_full.at[k], entering.at[k + 1, section], full_send.at[k],
                        back_recv.at[k + 1, section], half, seq,
                    ).wait_send()

        return carry

    lax.fori_loop(0, TICKS, tick, 0)
    back_sent(TICKS - 1)

    @pl.when(relays)
    def _():
        for t in range(TICKS - 1):
            for c in range(2):
                relay_wait(t, c).wait_send()

    for f in range(CHUNKS):
        piece = remote(
            entering.at[TICKS, f], entering.at[TICKS, f], back_send.at[0],
            back_recv.at[TICKS, f], slot, seq,
        )

        @pl.when(jnp.logical_or(zrow > 0, mine != f))
        def _():
            piece.wait_recv()

        out_ref[0, 0, :, f * CHUNK:(f + 1) * CHUNK] = entering[TICKS, f]


def local(*args):
    dma = pltpu.SemaphoreType.DMA
    vmem = pl.BlockSpec(memory_space=pltpu.VMEM)
    hbm = pl.BlockSpec(memory_space=pltpu.HBM)
    smem = pl.BlockSpec(memory_space=pltpu.SMEM)
    block = (CHUNKS, ROWS, CHUNK)
    return pl.pallas_call(
        kernel,
        out_shape=jax.ShapeDtypeStruct((1, 1, ROWS, WIDE), BF),
        in_specs=[hbm] * 10 + [smem],
        out_specs=vmem,
        scratch_shapes=[
            pltpu.VMEM((4, WIDE, WIDE), BF),
            pltpu.VMEM((2, 1, 512), F32),
            pltpu.VMEM((2, MIXES, 1, 512), F32),
            pltpu.VMEM((2, MIXES, 2, 512), F32),
            pltpu.VMEM((TICKS + 1,) + block, BF),
            pltpu.VMEM((TICKS, 3) + block, BF),
            pltpu.VMEM((4 * ROWS, WIDE), BF),
            pltpu.VMEM((ROWS, WIDE), BF),
            pltpu.VMEM((4 * ROWS, WIDE), BF),
            pltpu.VMEM((4 * ROWS, WIDE), BF),
            pltpu.VMEM((ROWS, WIDE), BF),
            pltpu.VMEM(block, BF),
            pltpu.VMEM((TICKS,) + block, BF),
            pltpu.VMEM(block, BF),
            pltpu.VMEM((TICKS, 4, 2, ROWS, CHUNK), BF),
            pltpu.VMEM(block, BF),
            pltpu.VMEM((MIXES, 2, ROWS, ROWS), BF),
            pltpu.VMEM((MIXES, 4, CHUNK), F32),
            pltpu.VMEM((2 * ROWS, 4 * ROWS), F32),
            pltpu.VMEM((TICKS - 1, 64, ROWS), BF),
            pltpu.VMEM((TICKS - 1, 64, ROWS), BF),
            pltpu.VMEM((TICKS - 1, ROWS, CHUNK), BF),
            pltpu.VMEM((MIXES, 8, ROWS), jnp.int32),
            pltpu.VMEM((TICKS - 1, 2, ROWS, CHUNK), BF),
            dma((CHUNKS,)), dma, dma, dma((TICKS - 1, 2)), dma((TICKS - 1, 2)),
            dma((4,)), dma((4,)), dma((4,)), dma((3,)), dma((3,)), dma((3,)),
            dma, dma, dma((TICKS - 1,)),
            dma((CHUNKS,)), dma((TICKS, CHUNKS)), dma((CHUNKS,)),
            dma((3, HALO_PARTS)), dma((TICKS, 3, HALO_PARTS)),
            dma((7,)), dma((TICKS, CHUNKS)),
            dma((3,)), dma((TICKS, 4)),
            dma((CHUNKS,)), dma((TICKS + 1, CHUNKS)),
        ],
        compiler_params=pltpu.CompilerParams(
            collective_id=0, has_side_effects=True, vmem_limit_bytes=60 * 1024 * 1024
        ),
    )(*args)


def solution(mesh):
    in_specs = (
        P("seq", "section", None, None),
        P(None, "seq", None, "section", None),
        P("section", None),
        P("section", None, None),
        P("section", None, None),
        P("section", None, None),
        P("section", None, None),
        P(None, "section", None),
        P("section", None, None, None),
        P(),
        P("seq", None, None),
    )
    out_specs = P("seq", "section", None, None)

    def run(start, fresh, gain, asking, lookup, content, emitting, turning, scaling, lines, table):
        return jax.shard_map(
            local, mesh=mesh, in_specs=in_specs, out_specs=out_specs, check_vma=False
        )(
            start, jnp.swapaxes(fresh, 3, 4), gain, asking, lookup, content, emitting,
            jnp.swapaxes(turning, 0, 1), scaling, jnp.swapaxes(lines, 0, 1), table,
        )

    return run
```

```python
import jax
import jax.numpy as jnp
from jax import lax
from jax.experimental import pallas as pl
from jax.experimental.pallas import tpu as pltpu
from jax.sharding import PartitionSpec as P

HEADS = 16
WIN = 3
MIXES = 5
TICKS = 3
FAR = 4
ROWS = 128
CHUNK = 128
CHUNKS = 8
WIDE = 1024
HALO_PARTS = 4
PER_PART = CHUNKS // HALO_PARTS
BF = jnp.bfloat16
F32 = jnp.float32


def remote(src, dst, send_sem, recv_sem, section, seq):
    return pltpu.make_async_remote_copy(
        src_ref=src,
        dst_ref=dst,
        send_sem=send_sem,
        recv_sem=recv_sem,
        device_id={"section": section, "seq": seq},
        device_id_type=pl.DeviceIdType.MESH,
    )


def kernel(
    start_ref, fresh_ref, gain_ref, wq_ref, wk_ref, wv_ref, wo_ref, angle_ref, scale_ref,
    pairing_ref, table_ref,
    out_ref,
    weights, gains, angles, scales, entering, halo, normed, queries, keys, values, attended,
    mixed, row_in, row_out, col_in, col_out, onehot, coef, bias, fresh_own, fresh_in, fresh_full,
    pairing, relay, ready,
    start_sem, pairing_sem, fresh_sem, relay_send, relay_recv,
    weight_local, weight_send, weight_recv, param_local, param_send, param_recv,
    fresh_send, fresh_recv, full_send,
    near_send, near_recv, ahead_send, halo_send, halo_recv, row_send, row_recv, col_send, col_recv, back_send, back_recv,
):
    slot = lax.axis_index("section")
    seq = lax.axis_index("seq")
    section = slot // 2
    half = slot % 2
    sister = slot + 1 - 2 * half
    x = seq % 4
    z = seq // 4
    zrow = z % 4
    zbase = z - zrow
    mine = 2 * x + half
    held = (zrow + x) % 4

    weight_refs = (wk_ref, wv_ref, wq_ref, wo_ref)
    place = pl.ds(pl.multiple_of(half * 512, 512), 512)
    local_weights = [
        pltpu.make_async_copy(ref.at[0], weights.at[k, place], weight_local.at[k])
        for k, ref in enumerate(weight_refs)
    ]
    param_pairs = (
        (gain_ref, gains.at[half]),
        (angle_ref, angles.at[half]),
        (scale_ref.at[0], scales.at[half]),
    )
    local_params = [
        pltpu.make_async_copy(src, dst, param_local.at[k]) for k, (src, dst) in enumerate(param_pairs)
    ]
    local_starts = [
        pltpu.make_async_copy(
            start_ref.at[0, 0, :, pl.ds(f * CHUNK, CHUNK)], entering.at[0, f], start_sem.at[f]
        )
        for f in range(CHUNKS)
    ]
    local_pairing = pltpu.make_async_copy(pairing_ref, pairing, pairing_sem)
    local_fresh = pltpu.make_async_copy(fresh_ref.at[:, 0, half], fresh_own, fresh_sem)
    for copy in local_starts + local_params + [local_pairing] + local_weights + [local_fresh]:
        copy.start()

    @pl.when(seq < 2)
    def _():
        halo[...] = jnp.zeros_like(halo)

    barrier = pltpu.get_barrier_semaphore()

    def greet(to_section, to_seq):
        pl.semaphore_signal(
            barrier, inc=1, device_id={"section": to_section, "seq": to_seq},
            device_id_type=pl.DeviceIdType.MESH,
        )

    for k in range(1, CHUNKS):
        peer = (mine + k) % CHUNKS
        greet(2 * section + peer % 2, 4 * z + peer // 2)
    for k in range(1, 4):
        greet(slot, 4 * (zbase + (zrow + k) % 4) + x)
    for k in range(CHUNKS):
        source = (mine + k) % CHUNKS
        source_seq = 4 * (zbase + (x - source // 2 + 4) % 4) + source // 2

        @pl.when(jnp.logical_and(section > 0, section != FAR))
        def _():
            greet(2 * section - 2 + source % 2, source_seq)

        if k == 0:
            @pl.when(zrow > 0)
            def _():
                greet(2 * section + source % 2, source_seq)
        else:
            greet(2 * section + source % 2, source_seq)

    @pl.when(seq > 0)
    def _():
        greet(slot, seq - 1)

    fed = jnp.logical_and(section != 0, section != FAR)
    crosses = jnp.logical_and(section == FAR - 1, x == 3)
    feeds = jnp.logical_and(section != 7, section != FAR - 1)
    before = jnp.maximum(seq - 1, 0)

    @pl.when(jnp.logical_and(fed, seq > 0))
    def _():
        for f in range(CHUNKS):
            row = (before % 4 - f // 2 + 4) % 4
            greet(2 * section - 2 + f % 2, 4 * (before // 16 * 4 + row) + f // 2)

    has_extra = jnp.logical_or(half == 1, seq >= 2)
    gives_extra = jnp.logical_or(half == 0, seq < 30)

    @pl.when(has_extra)
    def _():
        greet(sister, seq - 2 * (1 - half))

    @pl.when(section == 0)
    def _():
        for k in range(1, 8):
            greet(2 * k + half, seq)

    relays = section < 3
    relay_seq = 4 * (zbase + (x - section + 8) % 4) + section % 4

    @pl.when(relays)
    def _():
        for c in range(2):
            greet(2 * (FAR - 1) + c, relay_seq)

    @pl.when(relays)
    def _():
        greet(2 * FAR + half, seq)

    @pl.when(crosses)
    def _():
        for r in range(4):
            pair = 4 * (zbase + r) + held
            for c in range(2):
                greet(2 * FAR + c, pair)

    for copy in local_starts:
        copy.wait()

    one = jnp.int32(1)
    zero = jnp.int32(0)
    at_end = jnp.logical_and(held == 3, zbase == 4)
    expected = (
        7 + 3 + jnp.where(
            jnp.logical_and(section < 7, jnp.logical_not(crosses)), 8 * one, zero
        ) + 8 - jnp.where(zrow == 0, one, zero)
        + jnp.where(seq < 31, one, zero) + jnp.where(gives_extra, one, zero)
        + jnp.where(section > 0, one, zero)
        + jnp.where(section == FAR, 5 * one, zero)
        + jnp.where(feeds, 8 * one, zero)
        - jnp.where(jnp.logical_and(feeds, at_end), 2 * one, zero)
    )
    pl.semaphore_wait(barrier, expected)

    def answer(to_section, to_seq):
        pl.semaphore_signal(
            ready, inc=1, device_id={"section": to_section, "seq": to_seq},
            device_id_type=pl.DeviceIdType.MESH,
        )

    @pl.when(section == FAR)
    def _():
        for k in range(3):
            answer(2 * k + half, seq)
        for c in range(2):
            answer(2 * (FAR - 1) + c, 4 * (zbase + (x + 1) % 4) + 3)

    def near_copy(t, f, to_seq):
        return remote(
            entering.at[t, f], halo.at[t, half, f], near_send.at[f], near_recv.at[t, f],
            slot, to_seq,
        )

    def by_neighbor(t):
        return jnp.logical_or(t == 0, jnp.logical_not(fed))

    def forward_copy(t, part):
        span = pl.ds(PER_PART * part, PER_PART)
        return remote(
            halo.at[t, half, span], halo.at[t, half, span], halo_send.at[1, part],
            halo_recv.at[t, 1, part], sister, seq,
        )

    def forward_wait(t, part):
        span = pl.ds(PER_PART * part, PER_PART)
        return remote(
            halo.at[t, 1 - half, span], halo.at[t, 1 - half, span], halo_send.at[1, part],
            halo_recv.at[t, 1, part], sister, seq,
        )

    def extra_copy(t, part):
        span = pl.ds(PER_PART * part, PER_PART)
        return remote(
            entering.at[t, span], halo.at[t, 2, span], halo_send.at[2, part],
            halo_recv.at[t, 2, part], sister, seq + 2 * half,
        )

    def relay_copy(t, c):
        return remote(
            relay.at[t, c], entering.at[t + 1, 2 * section + c], relay_send.at[t, c],
            back_recv.at[t + 1, 2 * section + c], 2 * FAR + half, seq,
        )

    def enter_wait(t, f):
        remote(
            entering.at[t, f], entering.at[t, f], back_send.at[0], back_recv.at[t, f], slot, seq
        ).wait_recv()

    def relay_wait(t, c):
        return remote(
            relay.at[t, c], relay.at[t, c], relay_send.at[t, c], relay_recv.at[t, c], slot, seq
        )

    def send_halo(t, part):
        @pl.when(jnp.logical_and(seq < 31, by_neighbor(t)))
        def _():
            for c in range(PER_PART):
                near_copy(t, PER_PART * part + c, seq + 1).start()

        @pl.when(gives_extra)
        def _():
            extra_copy(t, part).start()

    param_copies = [
        remote(src, dst, param_send.at[k], param_recv.at[k], sister, seq)
        for k, (src, dst) in enumerate(param_pairs)
    ]
    weight_copies = [
        remote(ref.at[0], weights.at[k, place], weight_send.at[k], weight_recv.at[k], sister, seq)
        for k, ref in enumerate(weight_refs)
    ]
    other = pl.ds(pl.multiple_of((1 - half) * 512, 512), 512)
    fresh_copy = remote(
        fresh_ref.at[:, 0, 1 - half], fresh_in, fresh_send, fresh_recv, sister, seq
    )
    for copy in param_copies:
        copy.start()
    for part in range(HALO_PARTS):
        send_halo(0, part)
    for copy in weight_copies:
        copy.start()
    fresh_copy.start()

    row_num = lax.broadcasted_iota(jnp.int32, (ROWS, ROWS), 0)
    col_num = lax.broadcasted_iota(jnp.int32, (ROWS, ROWS), 1)
    local_pairing.wait()
    for layer in range(MIXES):
        lines = pairing[layer, pl.ds(section, 1), :]
        back = jnp.where(row_num == lines, F32(1), F32(0))
        onehot[layer, 0] = back.T.astype(BF)
        onehot[layer, 1] = back.astype(BF)

    drop = jnp.full((ROWS, ROWS), -1e30, F32)
    keep = jnp.zeros((ROWS, ROWS), F32)
    for place_num, reach in ((0, 2 + half), (1, 1 + half), (2, 3 - 2 * half)):
        seen = table_ref[0, half, reach - 1]
        inside = jnp.where(2 * seq + half - reach >= 0, one, zero)
        shown = jnp.full((ROWS, ROWS), seen * inside, jnp.int32)
        flags = jnp.where(shown == 1, keep, drop)
        bias[0:ROWS, place_num * ROWS:(place_num + 1) * ROWS] = flags
        bias[ROWS:2 * ROWS, place_num * ROWS:(place_num + 1) * ROWS] = flags
    causal = jnp.where(col_num <= row_num, keep, drop)
    bias[0:ROWS, 3 * ROWS:] = causal
    bias[ROWS:2 * ROWS, 3 * ROWS:] = causal

    for copy in local_params:
        copy.wait()
    for k, (_, dst) in enumerate(
        ((None, gains.at[1 - half]), (None, angles.at[1 - half]), (None, scales.at[1 - half]))
    ):
        remote(dst, dst, param_send.at[k], param_recv.at[k], sister, seq).wait_recv()
    feature_half = mine // 4
    features = pl.ds(pl.multiple_of((mine % 4) * CHUNK, CHUNK), CHUNK)
    angle = angles[feature_half, :, 0, features]
    cosine = jnp.cos(angle)
    sine = jnp.sin(angle)
    for layer in range(MIXES):
        scale = scales[feature_half, layer, :, features]
        c = cosine[layer:layer + 1]
        n = sine[layer:layer + 1]
        coef[layer, 0:1] = scale[0:1] * c
        coef[layer, 1:2] = scale[0:1] * n
        coef[layer, 2:3] = scale[1:2] * c
        coef[layer, 3:4] = scale[1:2] * n

    def norm(block, place_num):
        total = jnp.zeros((ROWS, 1), F32)
        for f in range(CHUNKS):
            wide = block[f].astype(F32)
            total = total + jnp.sum(wide * wide, axis=-1, keepdims=True)
        factor = lax.rsqrt(total * (1.0 / WIDE) + 1e-6)
        for f in range(CHUNKS):
            part = pl.ds((f % 4) * CHUNK, CHUNK)
            gain = gains[f // 4, :, part]
            normed[place_num * ROWS:(place_num + 1) * ROWS, f * CHUNK:(f + 1) * CHUNK] = (
                block[f].astype(F32) * factor * gain
            ).astype(BF)

    def project(which, rows, target, scale=None):
        def one_part(k, carry):
            cols = pl.ds(pl.multiple_of(k * 256, 256), 256)
            product = jnp.dot(
                normed[rows, :], weights[which, :, cols], preferred_element_type=F32
            )
            if scale is None:
                target[rows, cols] = product.astype(BF)
            else:
                target[:, cols] = (product * scale).astype(BF)
            return carry

        lax.fori_loop(0, 4, one_part, 0, unroll=4)

    def await_weight(t, which):
        @pl.when(t == 0)
        def _():
            local_weights[which].wait()
            remote(
                weights.at[which, other], weights.at[which, other], weight_send.at[which],
                weight_recv.at[which], sister, seq,
            ).wait_recv()

    def mix(layer, lower, upper):
        count = len(lower)
        low = jnp.concatenate(lower, axis=1)
        up = jnp.concatenate(upper, axis=1)
        rows = [
            jnp.concatenate([coef[layer, k:k + 1]] * count, axis=1) for k in range(4)
        ]
        to_low = jnp.dot(onehot[layer, 0], up, preferred_element_type=F32)
        to_up = jnp.dot(onehot[layer, 1], low, preferred_element_type=F32)
        new_low = (rows[0] * low.astype(F32) + rows[1] * to_low).astype(BF)
        new_up = (rows[2] * up.astype(F32) - rows[3] * to_up).astype(BF)
        cut = lambda whole: [whole[:, k * CHUNK:(k + 1) * CHUNK] for k in range(count)]
        return cut(new_low), cut(new_up)

    def mix_all(layer, bit, blocks):
        lows = [b for b in range(len(blocks)) if not b >> bit & 1]
        ups = [b | 1 << bit for b in lows]
        new_low, new_up = mix(layer, [blocks[b] for b in lows], [blocks[b] for b in ups])
        result = list(blocks)
        for k, b in enumerate(lows):
            result[b] = new_low[k]
        for k, b in enumerate(ups):
            result[b] = new_up[k]
        return result

    lane = lax.broadcasted_iota(jnp.int32, (1, CHUNK), 1)
    first_head = jnp.where(lane < 64, F32(1), F32(0))
    pick_first = first_head.astype(BF)
    pick_second = (1 - first_head).astype(BF)

    def ahead_copy(t, k, m):
        target = (zrow + k) % 4
        c = (half + m) % 2
        pair = 4 * (zbase + target) + held
        return pair, remote(
            col_out.at[2 * target + c], halo.at[t + 1, c, mine], ahead_send.at[2 * k + m],
            near_recv.at[t + 1, mine], 2 * section + 2 + c, jnp.minimum(pair + 1, 31),
        )

    def back_sent(t):
        @pl.when(jnp.logical_or(t == TICKS - 1, section < 7))
        def _():
            for k in range(4):
                for m in range(2):
                    target = (zrow + k) % 4
                    c = (half + m) % 2
                    sent = remote(
                        col_out.at[2 * target + c], entering.at[t + 1, mine],
                        back_send.at[2 * k + m], back_recv.at[t + 1, mine],
                        slot, seq,
                    )
                    if k or m:
                        sent.wait_send()
                    else:
                        @pl.when(jnp.logical_or(t < TICKS - 1, zrow > 0))
                        def _():
                            sent.wait_send()

        @pl.when(jnp.logical_and(feeds, t < TICKS - 1))
        def _():
            for k in range(4):
                for m in range(2):
                    pair, copy_ahead = ahead_copy(t, k, m)

                    @pl.when(pair < 31)
                    def _():
                        copy_ahead.wait_send()

    def tick(t, carry):
        for step in range(HALO_PARTS):
            part = (x - zrow + step + 4) % 4

            @pl.when(jnp.logical_and(t > 0, section > 0))
            def _():
                for c in range(PER_PART):
                    enter_wait(t, PER_PART * part + c)
                send_halo(t, part)

        norm(entering.at[t], 3)
        own_rows = pl.ds(3 * ROWS, ROWS)
        await_weight(t, 0)
        project(0, own_rows, keys)
        await_weight(t, 1)
        project(1, own_rows, values)
        await_weight(t, 2)
        project(2, own_rows, queries, scale=0.125)

        @pl.when(t == 0)
        def _():
            local_fresh.wait()
            fresh_copy.wait_recv()
            for k in range(TICKS - 1):
                own = fresh_own[k].astype(F32)
                theirs = fresh_in[k].astype(F32)
                even = jnp.concatenate([own, theirs], axis=0)
                odd = jnp.concatenate([theirs, own], axis=0)
                fresh_full[k] = jnp.where(half == 0, even, odd).T.astype(BF)

                @pl.when(section == 0)
                def _():
                    entering[k + 1, 0] = fresh_full[k]

                @pl.when(section > 0)
                def _():
                    remote(
                        fresh_full.at[k], entering.at[k + 1, section], full_send.at[k],
                        back_recv.at[k + 1, section], half, seq,
                    ).start()

        for step in range(HALO_PARTS):
            part = (before % 4 - before // 4 % 4 + step + 4) % 4

            @pl.when(seq > 0)
            def _():
                for c in range(PER_PART):
                    near_copy(t, PER_PART * part + c, seq).wait_recv()
                forward_copy(t, part).start()
        for part in range(HALO_PARTS):
            @pl.when(has_extra)
            def _():
                extra_copy(t, part).wait_recv()
        norm(halo.at[t, 2], 2)
        for part in range(HALO_PARTS):
            @pl.when(seq > 0)
            def _():
                forward_wait(t, part).wait_recv()
        norm(halo.at[t, 0], 0)
        norm(halo.at[t, 1], 1)
        near_rows = pl.ds(0, 3 * ROWS)
        project(0, near_rows, keys)
        project(1, near_rows, values)

        def two_heads(k, carry):
            cols = pl.ds(pl.multiple_of(k * CHUNK, CHUNK), CHUNK)
            both = queries[:, cols]
            stacked = jnp.concatenate([both * pick_first, both * pick_second], axis=0)
            scores = lax.dot_general(
                stacked, keys[:, cols], (((1,), (1,)), ((), ())), preferred_element_type=F32
            ) + bias[...]
            top = jnp.max(scores, axis=-1, keepdims=True)
            expo = jnp.exp(scores - top)
            total = jnp.sum(expo, axis=-1, keepdims=True)
            summed = jnp.dot(expo.astype(BF), values[:, cols], preferred_element_type=F32) / total
            attended[:, cols] = jnp.where(lane < 64, summed[:ROWS], summed[ROWS:]).astype(BF)
            return carry

        lax.fori_loop(0, CHUNKS, two_heads, 0, unroll=4)
        await_weight(t, 3)

        @pl.when(t > 0)
        def _():
            back_sent(t - 1)

        sends = []
        for away in (2, 1, 3, 0):
            target = (x + away) % 4
            cols = pl.ds(pl.multiple_of(target * 256, 256), 256)
            product = jnp.dot(attended[...], weights[3, :, cols], preferred_element_type=F32)
            for c in range(2):
                f = 2 * target + c
                mixed[f] = (
                    entering[t, f].astype(F32) + product[:, c * CHUNK:(c + 1) * CHUNK]
                ).astype(BF)
            if away:
                for c in range(2):
                    copy = remote(
                        mixed.at[2 * target + c], row_in.at[t, mine],
                        row_send.at[2 * away - 1 + c], row_recv.at[t, mine],
                        2 * section + c, 4 * z + target,
                    )
                    copy.start()
                    sends.append(copy)
            else:
                copy = remote(
                    mixed.at[2 * x + 1 - half], row_in.at[t, mine], row_send.at[0],
                    row_recv.at[t, mine], sister, seq,
                )
                copy.start()
                sends.append(copy)
        row_in[t, mine] = mixed[mine]
        for k in range(1, CHUNKS):
            source = (mine + k) % CHUNKS
            remote(
                row_in.at[t, source], row_in.at[t, source], row_send.at[0],
                row_recv.at[t, source], slot, seq,
            ).wait_recv()
        blocks = [row_in[t, b] for b in range(CHUNKS)]
        for layer in range(3):
            blocks = mix_all(layer, layer, blocks)
        for b in range(CHUNKS):
            row_out[b] = blocks[b]

        for k in (2, 1, 3):
            target = (zrow + k) % 4
            pair = (target + x) % 4
            copy = remote(
                row_out.at[pl.ds(2 * pair, 2)], col_in.at[t, zrow], col_send.at[k - 1],
                col_recv.at[t, zrow], slot, 4 * (zbase + target) + x,
            )
            copy.start()
            sends.append(copy)
        for c in range(2):
            col_in[t, zrow, c] = row_out[2 * held + c]
        for k in range(1, 4):
            source = (zrow + k) % 4
            remote(
                col_in.at[t, source], col_in.at[t, source], col_send.at[0],
                col_recv.at[t, source], slot, seq,
            ).wait_recv()
        blocks = [col_in[t, r, c] for r in range(4) for c in range(2)]
        for layer in range(3, MIXES):
            blocks = mix_all(layer, layer - 2, blocks)
        for b in range(CHUNKS):
            col_out[b] = blocks[b]

        ahead = jnp.where(t < TICKS - 1, one, zero)
        last = t == TICKS - 1
        by_relay = jnp.logical_and(jnp.logical_and(section == FAR - 1, x < 3), t < TICKS - 1)
        direct = jnp.logical_and(
            jnp.logical_or(last, section < 7), jnp.logical_not(by_relay)
        )
        @pl.when(jnp.logical_and(crosses, t == 0))
        def _():
            pl.semaphore_wait(ready, 8)

        for k in range(4):
            target = (zrow + k) % 4
            for m in range(2):
                c = (half + m) % 2

                def back_copy():
                    return remote(
                        col_out.at[2 * target + c], entering.at[t + 1, mine],
                        back_send.at[2 * k + m], back_recv.at[t + 1, mine],
                        2 * (section + ahead) + c, 4 * (zbase + target) + held,
                    )

                if k == 0 and m == 0:
                    itself = jnp.logical_and(t == TICKS - 1, zrow == 0)

                    @pl.when(itself)
                    def _():
                        entering[t + 1, mine] = col_out[2 * target + c]

                    @pl.when(jnp.logical_and(jnp.logical_not(itself), direct))
                    def _():
                        back_copy().start()
                else:
                    @pl.when(direct)
                    def _():
                        back_copy().start()

                @pl.when(by_relay)
                def _():
                    remote(
                        col_out.at[2 * target + c], relay.at[t, half],
                        back_send.at[2 * k + m], relay_recv.at[t, half],
                        2 * x + c, 4 * (zbase + target) + held,
                    ).start()

        @pl.when(jnp.logical_and(feeds, t < TICKS - 1))
        def _():
            for k in range(4):
                for m in range(2):
                    pair, copy_ahead = ahead_copy(t, k, m)

                    @pl.when(pair < 31)
                    def _():
                        copy_ahead.start()

        for part in range(HALO_PARTS):
            @pl.when(jnp.logical_and(seq < 31, by_neighbor(t)))
            def _():
                for c in range(PER_PART):
                    near_copy(t, PER_PART * part + c, seq + 1).wait_send()

            @pl.when(gives_extra)
            def _():
                extra_copy(t, part).wait_send()

            @pl.when(seq > 0)
            def _():
                forward_copy(t, part).wait_send()

        @pl.when(jnp.logical_and(section == 0, t < TICKS - 1))
        def _():
            for part in range(HALO_PARTS):
                for c in range(PER_PART):
                    if part or c:
                        enter_wait(t + 1, PER_PART * part + c)
                send_halo(t + 1, part)

        @pl.when(jnp.logical_and(relays, t < TICKS - 1))
        def _():
            @pl.when(t == 0)
            def _():
                pl.semaphore_wait(ready, 1)

            for c in range(2):
                relay_wait(t, c).wait_recv()
                relay_copy(t, c).start()

        for copy in sends:
            copy.wait_send()

        @pl.when(t == 0)
        def _():
            for copy in param_copies + weight_copies + [fresh_copy]:
                copy.wait_send()

            @pl.when(section > 0)
            def _():
                for k in range(TICKS - 1):
                    remote(
                        fresh_full.at[k], entering.at[k + 1, section], full_send.at[k],
                        back_recv.at[k + 1, section], half, seq,
                    ).wait_send()

        return carry

    lax.fori_loop(0, TICKS, tick, 0)
    back_sent(TICKS - 1)

    @pl.when(relays)
    def _():
        for t in range(TICKS - 1):
            for c in range(2):
                relay_copy(t, c).wait_send()

    for f in range(CHUNKS):
        piece = remote(
            entering.at[TICKS, f], entering.at[TICKS, f], back_send.at[0],
            back_recv.at[TICKS, f], slot, seq,
        )

        @pl.when(jnp.logical_or(zrow > 0, mine != f))
        def _():
            piece.wait_recv()

        out_ref[0, 0, :, f * CHUNK:(f + 1) * CHUNK] = entering[TICKS, f]


def local(*args):
    dma = pltpu.SemaphoreType.DMA
    vmem = pl.BlockSpec(memory_space=pltpu.VMEM)
    hbm = pl.BlockSpec(memory_space=pltpu.HBM)
    smem = pl.BlockSpec(memory_space=pltpu.SMEM)
    block = (CHUNKS, ROWS, CHUNK)
    return pl.pallas_call(
        kernel,
        out_shape=jax.ShapeDtypeStruct((1, 1, ROWS, WIDE), BF),
        in_specs=[hbm] * 10 + [smem],
        out_specs=vmem,
        scratch_shapes=[
            pltpu.VMEM((4, WIDE, WIDE), BF),
            pltpu.VMEM((2, 1, 512), F32),
            pltpu.VMEM((2, MIXES, 1, 512), F32),
            pltpu.VMEM((2, MIXES, 2, 512), F32),
            pltpu.VMEM((TICKS + 1,) + block, BF),
            pltpu.VMEM((TICKS, 3) + block, BF),
            pltpu.VMEM((4 * ROWS, WIDE), BF),
            pltpu.VMEM((ROWS, WIDE), BF),
            pltpu.VMEM((4 * ROWS, WIDE), BF),
            pltpu.VMEM((4 * ROWS, WIDE), BF),
            pltpu.VMEM((ROWS, WIDE), BF),
            pltpu.VMEM(block, BF),
            pltpu.VMEM((TICKS,) + block, BF),
            pltpu.VMEM(block, BF),
            pltpu.VMEM((TICKS, 4, 2, ROWS, CHUNK), BF),
            pltpu.VMEM(block, BF),
            pltpu.VMEM((MIXES, 2, ROWS, ROWS), BF),
            pltpu.VMEM((MIXES, 4, CHUNK), F32),
            pltpu.VMEM((2 * ROWS, 4 * ROWS), F32),
            pltpu.VMEM((TICKS - 1, 64, ROWS), BF),
            pltpu.VMEM((TICKS - 1, 64, ROWS), BF),
            pltpu.VMEM((TICKS - 1, ROWS, CHUNK), BF),
            pltpu.VMEM((MIXES, 8, ROWS), jnp.int32),
            pltpu.VMEM((TICKS - 1, 2, ROWS, CHUNK), BF),
            pltpu.SemaphoreType.REGULAR,
            dma((CHUNKS,)), dma, dma, dma((TICKS - 1, 2)), dma((TICKS - 1, 2)),
            dma((4,)), dma((4,)), dma((4,)), dma((3,)), dma((3,)), dma((3,)),
            dma, dma, dma((TICKS - 1,)),
            dma((CHUNKS,)), dma((TICKS, CHUNKS)), dma((CHUNKS,)),
            dma((3, HALO_PARTS)), dma((TICKS, 3, HALO_PARTS)),
            dma((7,)), dma((TICKS, CHUNKS)),
            dma((3,)), dma((TICKS, 4)),
            dma((CHUNKS,)), dma((TICKS + 1, CHUNKS)),
        ],
        compiler_params=pltpu.CompilerParams(
            collective_id=0, has_side_effects=True, vmem_limit_bytes=60 * 1024 * 1024
        ),
    )(*args)


def solution(mesh):
    in_specs = (
        P("seq", "section", None, None),
        P(None, "seq", None, "section", None),
        P("section", None),
        P("section", None, None),
        P("section", None, None),
        P("section", None, None),
        P("section", None, None),
        P(None, "section", None),
        P("section", None, None, None),
        P(),
        P("seq", None, None),
    )
    out_specs = P("seq", "section", None, None)

    def run(start, fresh, gain, asking, lookup, content, emitting, turning, scaling, lines, table):
        return jax.shard_map(
            local, mesh=mesh, in_specs=in_specs, out_specs=out_specs, check_vma=False
        )(
            start, jnp.swapaxes(fresh, 3, 4), gain, asking, lookup, content, emitting,
            jnp.swapaxes(turning, 0, 1), scaling, jnp.swapaxes(lines, 0, 1), table,
        )

    return run
```

```python
import jax
import jax.numpy as jnp
from jax import lax
from jax.experimental import pallas as pl
from jax.experimental.pallas import tpu as pltpu
from jax.sharding import PartitionSpec as P

HEADS = 16
WIN = 3
MIXES = 5
TICKS = 3
FAR = 4
ROWS = 128
CHUNK = 128
CHUNKS = 8
WIDE = 1024
HALO_PARTS = 4
PER_PART = CHUNKS // HALO_PARTS
BF = jnp.bfloat16
F32 = jnp.float32


def remote(src, dst, send_sem, recv_sem, section, seq):
    return pltpu.make_async_remote_copy(
        src_ref=src,
        dst_ref=dst,
        send_sem=send_sem,
        recv_sem=recv_sem,
        device_id={"section": section, "seq": seq},
        device_id_type=pl.DeviceIdType.MESH,
    )


def kernel(
    start_ref, fresh_ref, gain_ref, wq_ref, wk_ref, wv_ref, wo_ref, angle_ref, scale_ref,
    pairing_ref, table_ref,
    out_ref,
    weights, gains, angles, scales, entering, halo, normed, queries, keys, values, attended,
    mixed, row_in, row_out, col_in, col_out, onehot, coef, earlier, bias, fresh_own, fresh_in, fresh_full,
    pairing, relay, ready,
    start_sem, pairing_sem, fresh_sem, relay_send, relay_recv,
    weight_local, weight_send, weight_recv, param_local, param_send, param_recv,
    fresh_send, fresh_recv, full_send,
    near_send, near_recv, ahead_send, halo_send, halo_recv, row_send, row_recv, col_send, col_recv, back_send, back_recv,
):
    slot = lax.axis_index("section")
    seq = lax.axis_index("seq")
    section = slot // 2
    half = slot % 2
    sister = slot + 1 - 2 * half
    x = seq % 4
    z = seq // 4
    zrow = z % 4
    zbase = z - zrow
    mine = 2 * x + half
    held = (zrow + x) % 4

    weight_refs = (wk_ref, wv_ref, wq_ref, wo_ref)
    place = pl.ds(pl.multiple_of(half * 512, 512), 512)
    local_weights = [
        pltpu.make_async_copy(ref.at[0], weights.at[k, place], weight_local.at[k])
        for k, ref in enumerate(weight_refs)
    ]
    param_pairs = (
        (gain_ref, gains.at[half]),
        (angle_ref, angles.at[half]),
        (scale_ref.at[0], scales.at[half]),
    )
    local_params = [
        pltpu.make_async_copy(src, dst, param_local.at[k]) for k, (src, dst) in enumerate(param_pairs)
    ]
    local_starts = [
        pltpu.make_async_copy(
            start_ref.at[0, 0, :, pl.ds(f * CHUNK, CHUNK)], entering.at[0, f], start_sem.at[f]
        )
        for f in range(CHUNKS)
    ]
    local_pairing = pltpu.make_async_copy(pairing_ref, pairing, pairing_sem)
    local_fresh = pltpu.make_async_copy(fresh_ref.at[:, 0, half], fresh_own, fresh_sem)
    for copy in local_starts + local_params + [local_pairing] + local_weights + [local_fresh]:
        copy.start()

    barrier = pltpu.get_barrier_semaphore()

    def greet(to_section, to_seq):
        pl.semaphore_signal(
            barrier, inc=1, device_id={"section": to_section, "seq": to_seq},
            device_id_type=pl.DeviceIdType.MESH,
        )

    for k in range(1, CHUNKS):
        peer = (mine + k) % CHUNKS
        greet(2 * section + peer % 2, 4 * z + peer // 2)
    for k in range(1, 4):
        greet(slot, 4 * (zbase + (zrow + k) % 4) + x)
    for k in range(CHUNKS):
        source = (mine + k) % CHUNKS
        source_seq = 4 * (zbase + (x - source // 2 + 4) % 4) + source // 2

        @pl.when(jnp.logical_and(section > 0, section != FAR))
        def _():
            greet(2 * section - 2 + source % 2, source_seq)

        if k == 0:
            @pl.when(zrow > 0)
            def _():
                greet(2 * section + source % 2, source_seq)
        else:
            greet(2 * section + source % 2, source_seq)

    @pl.when(seq > 0)
    def _():
        greet(slot, seq - 1)

    fed = jnp.logical_and(section != 0, section != FAR)
    crosses = jnp.logical_and(section == FAR - 1, x == 3)
    feeds = jnp.logical_and(section != 7, section != FAR - 1)
    before = jnp.maximum(seq - 1, 0)

    @pl.when(jnp.logical_and(fed, seq > 0))
    def _():
        for f in range(CHUNKS):
            row = (before % 4 - f // 2 + 4) % 4
            greet(2 * section - 2 + f % 2, 4 * (before // 16 * 4 + row) + f // 2)

    has_extra = jnp.logical_or(half == 1, seq >= 2)
    gives_extra = jnp.logical_or(half == 0, seq < 30)

    @pl.when(has_extra)
    def _():
        greet(sister, seq - 2 * (1 - half))

    @pl.when(section == 0)
    def _():
        for k in range(1, 8):
            greet(2 * k + half, seq)

    relays = section < 3
    relay_seq = 4 * (zbase + (x - section + 8) % 4) + section % 4

    @pl.when(relays)
    def _():
        for c in range(2):
            greet(2 * (FAR - 1) + c, relay_seq)

    @pl.when(relays)
    def _():
        greet(2 * FAR + half, seq)

    @pl.when(crosses)
    def _():
        for r in range(4):
            pair = 4 * (zbase + r) + held
            for c in range(2):
                greet(2 * FAR + c, pair)

    blank = jnp.zeros((CHUNKS, ROWS, CHUNK), BF)

    @pl.when(seq == 0)
    def _():
        for t in range(TICKS):
            halo[t, 0] = blank
            halo[t, 1] = blank

    @pl.when(jnp.logical_not(has_extra))
    def _():
        for t in range(TICKS):
            halo[t, 2] = blank

    for copy in local_starts:
        copy.wait()

    one = jnp.int32(1)
    zero = jnp.int32(0)
    at_end = jnp.logical_and(held == 3, zbase == 4)
    expected = (
        7 + 3 + jnp.where(
            jnp.logical_and(section < 7, jnp.logical_not(crosses)), 8 * one, zero
        ) + 8 - jnp.where(zrow == 0, one, zero)
        + jnp.where(seq < 31, one, zero) + jnp.where(gives_extra, one, zero)
        + jnp.where(section > 0, one, zero)
        + jnp.where(section == FAR, 5 * one, zero)
        + jnp.where(feeds, 8 * one, zero)
        - jnp.where(jnp.logical_and(feeds, at_end), 2 * one, zero)
    )
    pl.semaphore_wait(barrier, expected)

    def answer(to_section, to_seq):
        pl.semaphore_signal(
            ready, inc=1, device_id={"section": to_section, "seq": to_seq},
            device_id_type=pl.DeviceIdType.MESH,
        )

    @pl.when(section == FAR)
    def _():
        for k in range(3):
            answer(2 * k + half, seq)
        for c in range(2):
            answer(2 * (FAR - 1) + c, 4 * (zbase + (x + 1) % 4) + 3)

    def near_copy(t, f, to_seq):
        return remote(
            entering.at[t, f], halo.at[t, half, f], near_send.at[f], near_recv.at[t, f],
            slot, to_seq,
        )

    def by_neighbor(t):
        return jnp.logical_or(t == 0, jnp.logical_not(fed))

    def forward_copy(t, part):
        span = pl.ds(PER_PART * part, PER_PART)
        return remote(
            halo.at[t, half, span], halo.at[t, half, span], halo_send.at[1, part],
            halo_recv.at[t, 1, part], sister, seq,
        )

    def forward_wait(t, part):
        span = pl.ds(PER_PART * part, PER_PART)
        return remote(
            halo.at[t, 1 - half, span], halo.at[t, 1 - half, span], halo_send.at[1, part],
            halo_recv.at[t, 1, part], sister, seq,
        )

    def extra_copy(t, part):
        span = pl.ds(PER_PART * part, PER_PART)
        return remote(
            entering.at[t, span], halo.at[t, 2, span], halo_send.at[2, part],
            halo_recv.at[t, 2, part], sister, seq + 2 * half,
        )

    def relay_copy(t, c):
        return remote(
            relay.at[t, c], entering.at[t + 1, 2 * section + c], relay_send.at[t, c],
            back_recv.at[t + 1, 2 * section + c], 2 * FAR + half, seq,
        )

    def enter_wait(t, f):
        remote(
            entering.at[t, f], entering.at[t, f], back_send.at[0], back_recv.at[t, f], slot, seq
        ).wait_recv()

    def relay_wait(t, c):
        return remote(
            relay.at[t, c], relay.at[t, c], relay_send.at[t, c], relay_recv.at[t, c], slot, seq
        )

    def send_halo(t, part):
        @pl.when(jnp.logical_and(seq < 31, by_neighbor(t)))
        def _():
            for c in range(PER_PART):
                near_copy(t, PER_PART * part + c, seq + 1).start()

        @pl.when(gives_extra)
        def _():
            extra_copy(t, part).start()

    param_copies = [
        remote(src, dst, param_send.at[k], param_recv.at[k], sister, seq)
        for k, (src, dst) in enumerate(param_pairs)
    ]
    weight_copies = [
        remote(ref.at[0], weights.at[k, place], weight_send.at[k], weight_recv.at[k], sister, seq)
        for k, ref in enumerate(weight_refs)
    ]
    other = pl.ds(pl.multiple_of((1 - half) * 512, 512), 512)
    fresh_copy = remote(
        fresh_ref.at[:, 0, 1 - half], fresh_in, fresh_send, fresh_recv, sister, seq
    )
    for copy in param_copies:
        copy.start()
    for part in range(HALO_PARTS):
        send_halo(0, part)
    for copy in weight_copies:
        copy.start()
    fresh_copy.start()

    row_num = lax.broadcasted_iota(jnp.int32, (ROWS, ROWS), 0)
    col_num = lax.broadcasted_iota(jnp.int32, (ROWS, ROWS), 1)
    local_pairing.wait()
    for layer in range(MIXES):
        lines = pairing[layer, pl.ds(section, 1), :]
        back = jnp.where(row_num == lines, F32(1), F32(0))
        onehot[layer, 0] = back.T.astype(BF)
        onehot[layer, 1] = back.astype(BF)

    drop = jnp.full((1, ROWS), -1e30, F32)
    keep = jnp.zeros((1, ROWS), F32)
    for place_num, reach in ((0, 1 + 2 * half), (1, 2), (2, 3 - 2 * half)):
        seen = table_ref[0, half, reach - 1]
        inside = jnp.where(2 * seq + half - reach >= 0, one, zero)
        shown = jnp.full((1, ROWS), seen * inside, jnp.int32)
        earlier[:, place_num * ROWS:(place_num + 1) * ROWS] = jnp.where(shown == 1, keep, drop)
    causal = jnp.where(col_num <= row_num, F32(0), F32(-1e30))
    bias[0:ROWS] = causal
    bias[ROWS:2 * ROWS] = causal

    for copy in local_params:
        copy.wait()
    for k, (_, dst) in enumerate(
        ((None, gains.at[1 - half]), (None, angles.at[1 - half]), (None, scales.at[1 - half]))
    ):
        remote(dst, dst, param_send.at[k], param_recv.at[k], sister, seq).wait_recv()
    feature_half = mine // 4
    features = pl.ds(pl.multiple_of((mine % 4) * CHUNK, CHUNK), CHUNK)
    angle = angles[feature_half, :, 0, features]
    cosine = jnp.cos(angle)
    sine = jnp.sin(angle)
    for layer in range(MIXES):
        scale = scales[feature_half, layer, :, features]
        c = cosine[layer:layer + 1]
        n = sine[layer:layer + 1]
        coef[layer, 0:1] = scale[0:1] * c
        coef[layer, 1:2] = scale[0:1] * n
        coef[layer, 2:3] = scale[1:2] * c
        coef[layer, 3:4] = scale[1:2] * n

    def norm(block, place_num):
        total = jnp.zeros((ROWS, 1), F32)
        for f in range(CHUNKS):
            wide = block[f].astype(F32)
            total = total + jnp.sum(wide * wide, axis=-1, keepdims=True)
        factor = lax.rsqrt(total * (1.0 / WIDE) + 1e-6)
        for f in range(CHUNKS):
            part = pl.ds((f % 4) * CHUNK, CHUNK)
            gain = gains[f // 4, :, part]
            normed[place_num * ROWS:(place_num + 1) * ROWS, f * CHUNK:(f + 1) * CHUNK] = (
                block[f].astype(F32) * factor * gain
            ).astype(BF)

    def project(which, rows, target, scale=None):
        def one_part(k, carry):
            cols = pl.ds(pl.multiple_of(k * 256, 256), 256)
            product = jnp.dot(
                normed[rows, :], weights[which, :, cols], preferred_element_type=F32
            )
            if scale is None:
                target[rows, cols] = product.astype(BF)
            else:
                target[:, cols] = (product * scale).astype(BF)
            return carry

        lax.fori_loop(0, 4, one_part, 0, unroll=4)

    def await_weight(t, which):
        @pl.when(t == 0)
        def _():
            local_weights[which].wait()
            remote(
                weights.at[which, other], weights.at[which, other], weight_send.at[which],
                weight_recv.at[which], sister, seq,
            ).wait_recv()

    def mix(layer, lower, upper):
        count = len(lower)
        low = jnp.concatenate(lower, axis=1)
        up = jnp.concatenate(upper, axis=1)
        rows = [
            jnp.concatenate([coef[layer, k:k + 1]] * count, axis=1) for k in range(4)
        ]
        to_low = jnp.dot(onehot[layer, 0], up, preferred_element_type=F32)
        to_up = jnp.dot(onehot[layer, 1], low, preferred_element_type=F32)
        new_low = (rows[0] * low.astype(F32) + rows[1] * to_low).astype(BF)
        new_up = (rows[2] * up.astype(F32) - rows[3] * to_up).astype(BF)
        cut = lambda whole: [whole[:, k * CHUNK:(k + 1) * CHUNK] for k in range(count)]
        return cut(new_low), cut(new_up)

    def mix_all(layer, bit, blocks):
        lows = [b for b in range(len(blocks)) if not b >> bit & 1]
        ups = [b | 1 << bit for b in lows]
        new_low, new_up = mix(layer, [blocks[b] for b in lows], [blocks[b] for b in ups])
        result = list(blocks)
        for k, b in enumerate(lows):
            result[b] = new_low[k]
        for k, b in enumerate(ups):
            result[b] = new_up[k]
        return result

    lane = lax.broadcasted_iota(jnp.int32, (1, CHUNK), 1)
    first_head = jnp.where(lane < 64, F32(1), F32(0))
    pick_first = first_head.astype(BF)
    pick_second = (1 - first_head).astype(BF)

    def ahead_copy(t, k, m):
        target = (zrow + k) % 4
        c = (half + m) % 2
        pair = 4 * (zbase + target) + held
        return pair, remote(
            col_out.at[2 * target + c], halo.at[t + 1, c, mine], ahead_send.at[2 * k + m],
            near_recv.at[t + 1, mine], 2 * section + 2 + c, jnp.minimum(pair + 1, 31),
        )

    def back_sent(t):
        @pl.when(jnp.logical_or(t == TICKS - 1, section < 7))
        def _():
            for k in range(4):
                for m in range(2):
                    target = (zrow + k) % 4
                    c = (half + m) % 2
                    sent = remote(
                        col_out.at[2 * target + c], entering.at[t + 1, mine],
                        back_send.at[2 * k + m], back_recv.at[t + 1, mine],
                        slot, seq,
                    )
                    if k or m:
                        sent.wait_send()
                    else:
                        @pl.when(jnp.logical_or(t < TICKS - 1, zrow > 0))
                        def _():
                            sent.wait_send()

        @pl.when(jnp.logical_and(feeds, t < TICKS - 1))
        def _():
            for k in range(4):
                for m in range(2):
                    pair, copy_ahead = ahead_copy(t, k, m)

                    @pl.when(pair < 31)
                    def _():
                        copy_ahead.wait_send()

    ones = jnp.ones((4 * ROWS, CHUNK), BF)

    def tick(t, carry):
        for step in range(HALO_PARTS):
            part = (x - zrow + step + 4) % 4

            @pl.when(jnp.logical_and(t > 0, section > 0))
            def _():
                for c in range(PER_PART):
                    enter_wait(t, PER_PART * part + c)
                send_halo(t, part)

        norm(entering.at[t], 3)
        own_rows = pl.ds(3 * ROWS, ROWS)
        await_weight(t, 0)
        project(0, own_rows, keys)
        await_weight(t, 1)
        project(1, own_rows, values)
        await_weight(t, 2)
        project(2, own_rows, queries, scale=0.125)

        @pl.when(t == 0)
        def _():
            local_fresh.wait()
            fresh_copy.wait_recv()
            for k in range(TICKS - 1):
                own = fresh_own[k].astype(F32)
                theirs = fresh_in[k].astype(F32)
                even = jnp.concatenate([own, theirs], axis=0)
                odd = jnp.concatenate([theirs, own], axis=0)
                fresh_full[k] = jnp.where(half == 0, even, odd).T.astype(BF)

                @pl.when(section == 0)
                def _():
                    entering[k + 1, 0] = fresh_full[k]

                @pl.when(section > 0)
                def _():
                    remote(
                        fresh_full.at[k], entering.at[k + 1, section], full_send.at[k],
                        back_recv.at[k + 1, section], half, seq,
                    ).start()

        for step in range(HALO_PARTS):
            part = (before % 4 - before // 4 % 4 + step + 4) % 4

            @pl.when(seq > 0)
            def _():
                for c in range(PER_PART):
                    near_copy(t, PER_PART * part + c, seq).wait_recv()
                forward_copy(t, part).start()
        for part in range(HALO_PARTS):
            @pl.when(has_extra)
            def _():
                extra_copy(t, part).wait_recv()
        norm(halo.at[t, 2], 2)
        norm(halo.at[t, half], 1)
        middle_rows = pl.ds(ROWS, 2 * ROWS)
        project(0, middle_rows, keys)
        project(1, middle_rows, values)
        for part in range(HALO_PARTS):
            @pl.when(seq > 0)
            def _():
                forward_wait(t, part).wait_recv()
        norm(halo.at[t, 1 - half], 0)
        first_rows = pl.ds(0, ROWS)
        project(0, first_rows, keys)
        project(1, first_rows, values)

        def two_heads(k, carry):
            cols = pl.ds(pl.multiple_of(k * CHUNK, CHUNK), CHUNK)
            both = queries[:, cols]
            stacked = jnp.concatenate([both * pick_first, both * pick_second], axis=0)
            scores = lax.dot_general(
                stacked, keys[:, cols], (((1,), (1,)), ((), ())), preferred_element_type=F32
            )
            scores = jnp.concatenate(
                [scores[:, :3 * ROWS] + earlier[...], scores[:, 3 * ROWS:] + bias[...]], axis=1
            )
            top = jnp.max(scores, axis=-1, keepdims=True)
            expo = jnp.exp(scores - top).astype(BF)
            with_ones = jnp.concatenate([values[:, cols], ones], axis=1)
            product = jnp.dot(expo, with_ones, preferred_element_type=F32)
            summed = product[:, :CHUNK] / product[:, CHUNK:]
            attended[:, cols] = jnp.where(lane < 64, summed[:ROWS], summed[ROWS:]).astype(BF)
            return carry

        lax.fori_loop(0, CHUNKS, two_heads, 0, unroll=8)
        await_weight(t, 3)

        @pl.when(t > 0)
        def _():
            back_sent(t - 1)

        sends = []
        for away in (2, 1, 3, 0):
            target = (x + away) % 4
            cols = pl.ds(pl.multiple_of(target * 256, 256), 256)
            product = jnp.dot(attended[...], weights[3, :, cols], preferred_element_type=F32)
            for c in range(2):
                f = 2 * target + c
                mixed[f] = (
                    entering[t, f].astype(F32) + product[:, c * CHUNK:(c + 1) * CHUNK]
                ).astype(BF)
            if away:
                for c in range(2):
                    copy = remote(
                        mixed.at[2 * target + c], row_in.at[t, mine],
                        row_send.at[2 * away - 1 + c], row_recv.at[t, mine],
                        2 * section + c, 4 * z + target,
                    )
                    copy.start()
                    sends.append(copy)
            else:
                copy = remote(
                    mixed.at[2 * x + 1 - half], row_in.at[t, mine], row_send.at[0],
                    row_recv.at[t, mine], sister, seq,
                )
                copy.start()
                sends.append(copy)
        row_in[t, mine] = mixed[mine]
        for k in range(1, CHUNKS):
            source = (mine + k) % CHUNKS
            remote(
                row_in.at[t, source], row_in.at[t, source], row_send.at[0],
                row_recv.at[t, source], slot, seq,
            ).wait_recv()
        blocks = [row_in[t, b] for b in range(CHUNKS)]
        for layer in range(3):
            blocks = mix_all(layer, layer, blocks)
        for b in range(CHUNKS):
            row_out[b] = blocks[b]

        for k in (2, 1, 3):
            target = (zrow + k) % 4
            pair = (target + x) % 4
            copy = remote(
                row_out.at[pl.ds(2 * pair, 2)], col_in.at[t, zrow], col_send.at[k - 1],
                col_recv.at[t, zrow], slot, 4 * (zbase + target) + x,
            )
            copy.start()
            sends.append(copy)
        for c in range(2):
            col_in[t, zrow, c] = row_out[2 * held + c]
        for k in range(1, 4):
            source = (zrow + k) % 4
            remote(
                col_in.at[t, source], col_in.at[t, source], col_send.at[0],
                col_recv.at[t, source], slot, seq,
            ).wait_recv()
        blocks = [col_in[t, r, c] for r in range(4) for c in range(2)]
        for layer in range(3, MIXES):
            blocks = mix_all(layer, layer - 2, blocks)
        for b in range(CHUNKS):
            col_out[b] = blocks[b]

        ahead = jnp.where(t < TICKS - 1, one, zero)
        last = t == TICKS - 1
        by_relay = jnp.logical_and(jnp.logical_and(section == FAR - 1, x < 3), t < TICKS - 1)
        direct = jnp.logical_and(
            jnp.logical_or(last, section < 7), jnp.logical_not(by_relay)
        )
        @pl.when(jnp.logical_and(crosses, t == 0))
        def _():
            pl.semaphore_wait(ready, 8)

        for k in range(4):
            target = (zrow + k) % 4
            for m in range(2):
                c = (half + m) % 2

                def back_copy():
                    return remote(
                        col_out.at[2 * target + c], entering.at[t + 1, mine],
                        back_send.at[2 * k + m], back_recv.at[t + 1, mine],
                        2 * (section + ahead) + c, 4 * (zbase + target) + held,
                    )

                if k == 0 and m == 0:
                    itself = jnp.logical_and(t == TICKS - 1, zrow == 0)

                    @pl.when(itself)
                    def _():
                        entering[t + 1, mine] = col_out[2 * target + c]

                    @pl.when(jnp.logical_and(jnp.logical_not(itself), direct))
                    def _():
                        back_copy().start()
                else:
                    @pl.when(direct)
                    def _():
                        back_copy().start()

                @pl.when(by_relay)
                def _():
                    remote(
                        col_out.at[2 * target + c], relay.at[t, half],
                        back_send.at[2 * k + m], relay_recv.at[t, half],
                        2 * x + c, 4 * (zbase + target) + held,
                    ).start()

        @pl.when(jnp.logical_and(feeds, t < TICKS - 1))
        def _():
            for k in range(4):
                for m in range(2):
                    pair, copy_ahead = ahead_copy(t, k, m)

                    @pl.when(pair < 31)
                    def _():
                        copy_ahead.start()

        for part in range(HALO_PARTS):
            @pl.when(jnp.logical_and(seq < 31, by_neighbor(t)))
            def _():
                for c in range(PER_PART):
                    near_copy(t, PER_PART * part + c, seq + 1).wait_send()

            @pl.when(gives_extra)
            def _():
                extra_copy(t, part).wait_send()

            @pl.when(seq > 0)
            def _():
                forward_copy(t, part).wait_send()

        @pl.when(jnp.logical_and(section == 0, t < TICKS - 1))
        def _():
            for part in range(HALO_PARTS):
                for c in range(PER_PART):
                    if part or c:
                        enter_wait(t + 1, PER_PART * part + c)
                send_halo(t + 1, part)

        @pl.when(jnp.logical_and(relays, t < TICKS - 1))
        def _():
            @pl.when(t == 0)
            def _():
                pl.semaphore_wait(ready, 1)

            for c in range(2):
                relay_wait(t, c).wait_recv()
                relay_copy(t, c).start()

        for copy in sends:
            copy.wait_send()

        @pl.when(t == 0)
        def _():
            for copy in param_copies + weight_copies + [fresh_copy]:
                copy.wait_send()

            @pl.when(section > 0)
            def _():
                for k in range(TICKS - 1):
                    remote(
                        fresh_full.at[k], entering.at[k + 1, section], full_send.at[k],
                        back_recv.at[k + 1, section], half, seq,
                    ).wait_send()

        return carry

    lax.fori_loop(0, TICKS, tick, 0)
    back_sent(TICKS - 1)

    @pl.when(relays)
    def _():
        for t in range(TICKS - 1):
            for c in range(2):
                relay_copy(t, c).wait_send()

    for f in range(CHUNKS):
        piece = remote(
            entering.at[TICKS, f], entering.at[TICKS, f], back_send.at[0],
            back_recv.at[TICKS, f], slot, seq,
        )

        @pl.when(jnp.logical_or(zrow > 0, mine != f))
        def _():
            piece.wait_recv()

        out_ref[0, 0, :, f * CHUNK:(f + 1) * CHUNK] = entering[TICKS, f]


def local(*args):
    dma = pltpu.SemaphoreType.DMA
    vmem = pl.BlockSpec(memory_space=pltpu.VMEM)
    hbm = pl.BlockSpec(memory_space=pltpu.HBM)
    smem = pl.BlockSpec(memory_space=pltpu.SMEM)
    block = (CHUNKS, ROWS, CHUNK)
    return pl.pallas_call(
        kernel,
        out_shape=jax.ShapeDtypeStruct((1, 1, ROWS, WIDE), BF),
        in_specs=[hbm] * 10 + [smem],
        out_specs=vmem,
        scratch_shapes=[
            pltpu.VMEM((4, WIDE, WIDE), BF),
            pltpu.VMEM((2, 1, 512), F32),
            pltpu.VMEM((2, MIXES, 1, 512), F32),
            pltpu.VMEM((2, MIXES, 2, 512), F32),
            pltpu.VMEM((TICKS + 1,) + block, BF),
            pltpu.VMEM((TICKS, 3) + block, BF),
            pltpu.VMEM((4 * ROWS, WIDE), BF),
            pltpu.VMEM((ROWS, WIDE), BF),
            pltpu.VMEM((4 * ROWS, WIDE), BF),
            pltpu.VMEM((4 * ROWS, WIDE), BF),
            pltpu.VMEM((ROWS, WIDE), BF),
            pltpu.VMEM(block, BF),
            pltpu.VMEM((TICKS,) + block, BF),
            pltpu.VMEM(block, BF),
            pltpu.VMEM((TICKS, 4, 2, ROWS, CHUNK), BF),
            pltpu.VMEM(block, BF),
            pltpu.VMEM((MIXES, 2, ROWS, ROWS), BF),
            pltpu.VMEM((MIXES, 4, CHUNK), F32),
            pltpu.VMEM((1, 3 * ROWS), F32),
            pltpu.VMEM((2 * ROWS, ROWS), F32),
            pltpu.VMEM((TICKS - 1, 64, ROWS), BF),
            pltpu.VMEM((TICKS - 1, 64, ROWS), BF),
            pltpu.VMEM((TICKS - 1, ROWS, CHUNK), BF),
            pltpu.VMEM((MIXES, 8, ROWS), jnp.int32),
            pltpu.VMEM((TICKS - 1, 2, ROWS, CHUNK), BF),
            pltpu.SemaphoreType.REGULAR,
            dma((CHUNKS,)), dma, dma, dma((TICKS - 1, 2)), dma((TICKS - 1, 2)),
            dma((4,)), dma((4,)), dma((4,)), dma((3,)), dma((3,)), dma((3,)),
            dma, dma, dma((TICKS - 1,)),
            dma((CHUNKS,)), dma((TICKS, CHUNKS)), dma((CHUNKS,)),
            dma((3, HALO_PARTS)), dma((TICKS, 3, HALO_PARTS)),
            dma((7,)), dma((TICKS, CHUNKS)),
            dma((3,)), dma((TICKS, 4)),
            dma((CHUNKS,)), dma((TICKS + 1, CHUNKS)),
        ],
        compiler_params=pltpu.CompilerParams(
            collective_id=0, has_side_effects=True, vmem_limit_bytes=60 * 1024 * 1024
        ),
    )(*args)


def solution(mesh):
    in_specs = (
        P("seq", "section", None, None),
        P(None, "seq", None, "section", None),
        P("section", None),
        P("section", None, None),
        P("section", None, None),
        P("section", None, None),
        P("section", None, None),
        P(None, "section", None),
        P("section", None, None, None),
        P(),
        P("seq", None, None),
    )
    out_specs = P("seq", "section", None, None)

    def run(start, fresh, gain, asking, lookup, content, emitting, turning, scaling, lines, table):
        return jax.shard_map(
            local, mesh=mesh, in_specs=in_specs, out_specs=out_specs, check_vma=False
        )(
            start, jnp.swapaxes(fresh, 3, 4), gain, asking, lookup, content, emitting,
            jnp.swapaxes(turning, 0, 1), scaling, jnp.swapaxes(lines, 0, 1), table,
        )

    return run
```

```python
import jax
import jax.numpy as jnp
from jax import lax
from jax.experimental import pallas as pl
from jax.experimental.pallas import tpu as pltpu
from jax.sharding import PartitionSpec as P

HEADS = 16
WIN = 3
MIXES = 5
TICKS = 3
FAR = 4
ROWS = 128
CHUNK = 128
CHUNKS = 8
WIDE = 1024
HALO_PARTS = 4
PER_PART = CHUNKS // HALO_PARTS
BF = jnp.bfloat16
F32 = jnp.float32


def remote(src, dst, send_sem, recv_sem, section, seq):
    return pltpu.make_async_remote_copy(
        src_ref=src,
        dst_ref=dst,
        send_sem=send_sem,
        recv_sem=recv_sem,
        device_id={"section": section, "seq": seq},
        device_id_type=pl.DeviceIdType.MESH,
    )


def kernel(
    start_ref, fresh_ref, gain_ref, wq_ref, wk_ref, wv_ref, wo_ref, angle_ref, scale_ref,
    pairing_ref, table_ref,
    out_ref,
    weights, gains, angles, scales, entering, halo, normed, queries, keys, values, attended,
    mixed, row_in, row_out, col_in, col_out, onehot, coef, earlier, bias, fresh_own, fresh_in, fresh_full,
    pairing, relay, ready,
    start_sem, pairing_sem, fresh_sem, relay_send, relay_recv,
    weight_local, weight_send, weight_recv, param_local, param_send, param_recv,
    fresh_send, fresh_recv, full_send,
    near_send, near_recv, ahead_send, halo_send, halo_recv, row_send, row_recv, col_send, col_recv, back_send, back_recv,
):
    slot = lax.axis_index("section")
    seq = lax.axis_index("seq")
    section = slot // 2
    half = slot % 2
    sister = slot + 1 - 2 * half
    x = seq % 4
    z = seq // 4
    zrow = z % 4
    zbase = z - zrow
    mine = 2 * x + half
    held = (zrow + x) % 4

    weight_refs = (wk_ref, wv_ref, wq_ref, wo_ref)
    place = pl.ds(pl.multiple_of(half * 512, 512), 512)
    local_weights = [
        pltpu.make_async_copy(ref.at[0], weights.at[k, place], weight_local.at[k])
        for k, ref in enumerate(weight_refs)
    ]
    param_pairs = (
        (gain_ref, gains.at[half]),
        (angle_ref, angles.at[half]),
        (scale_ref.at[0], scales.at[half]),
    )
    local_params = [
        pltpu.make_async_copy(src, dst, param_local.at[k]) for k, (src, dst) in enumerate(param_pairs)
    ]
    local_starts = [
        pltpu.make_async_copy(
            start_ref.at[0, 0, :, pl.ds(f * CHUNK, CHUNK)], entering.at[0, f], start_sem.at[f]
        )
        for f in range(CHUNKS)
    ]
    local_pairing = pltpu.make_async_copy(pairing_ref, pairing, pairing_sem)
    local_fresh = pltpu.make_async_copy(fresh_ref.at[:, 0, half], fresh_own, fresh_sem)
    for copy in local_starts + local_params + [local_pairing] + local_weights + [local_fresh]:
        copy.start()

    barrier = pltpu.get_barrier_semaphore()

    def greet(to_section, to_seq):
        pl.semaphore_signal(
            barrier, inc=1, device_id={"section": to_section, "seq": to_seq},
            device_id_type=pl.DeviceIdType.MESH,
        )

    for k in range(1, CHUNKS):
        peer = (mine + k) % CHUNKS
        greet(2 * section + peer % 2, 4 * z + peer // 2)
    for k in range(1, 4):
        greet(slot, 4 * (zbase + (zrow + k) % 4) + x)
    for k in range(CHUNKS):
        source = (mine + k) % CHUNKS
        source_seq = 4 * (zbase + (x - source // 2 + 4) % 4) + source // 2

        @pl.when(jnp.logical_and(section > 0, section != FAR))
        def _():
            greet(2 * section - 2 + source % 2, source_seq)

        if k == 0:
            @pl.when(zrow > 0)
            def _():
                greet(2 * section + source % 2, source_seq)
        else:
            greet(2 * section + source % 2, source_seq)

    @pl.when(seq > 0)
    def _():
        greet(slot, seq - 1)

    fed = jnp.logical_and(section != 0, section != FAR)
    crosses = jnp.logical_and(section == FAR - 1, x == 3)
    feeds = jnp.logical_and(section != 7, section != FAR - 1)
    before = jnp.maximum(seq - 1, 0)

    @pl.when(jnp.logical_and(jnp.logical_and(fed, half == 1), seq > 0))
    def _():
        for f in range(CHUNKS):
            row = (before % 4 - f // 2 + 4) % 4
            greet(2 * section - 2 + f % 2, 4 * (before // 16 * 4 + row) + f // 2)

    has_extra = jnp.logical_or(half == 1, seq >= 2)
    gives_extra = jnp.logical_or(half == 0, seq < 30)

    @pl.when(has_extra)
    def _():
        greet(sister, seq - 2 * (1 - half))

    @pl.when(section == 0)
    def _():
        for k in range(1, 8):
            greet(2 * k + half, seq)

    relays = section < 3
    relay_seq = 4 * (zbase + (x - section + 8) % 4) + section % 4

    @pl.when(relays)
    def _():
        for c in range(2):
            greet(2 * (FAR - 1) + c, relay_seq)

    @pl.when(relays)
    def _():
        greet(2 * FAR + half, seq)

    @pl.when(crosses)
    def _():
        for r in range(4):
            pair = 4 * (zbase + r) + held
            for c in range(2):
                greet(2 * FAR + c, pair)

    blank = jnp.zeros((CHUNKS, ROWS, CHUNK), BF)

    @pl.when(seq == 0)
    def _():
        for t in range(TICKS):
            halo[t, 0] = blank
            halo[t, 1] = blank

    @pl.when(jnp.logical_not(has_extra))
    def _():
        for t in range(TICKS):
            halo[t, 2] = blank

    for copy in local_starts:
        copy.wait()

    one = jnp.int32(1)
    zero = jnp.int32(0)
    at_end = jnp.logical_and(held == 3, zbase == 4)
    expected = (
        7 + 3 + jnp.where(
            jnp.logical_and(section < 7, jnp.logical_not(crosses)), 8 * one, zero
        ) + 8 - jnp.where(zrow == 0, one, zero)
        + jnp.where(seq < 31, one, zero) + jnp.where(gives_extra, one, zero)
        + jnp.where(section > 0, one, zero)
        + jnp.where(section == FAR, 5 * one, zero)
        + jnp.where(feeds, 4 * one, zero)
        - jnp.where(jnp.logical_and(feeds, at_end), one, zero)
    )
    pl.semaphore_wait(barrier, expected)

    def answer(to_section, to_seq):
        pl.semaphore_signal(
            ready, inc=1, device_id={"section": to_section, "seq": to_seq},
            device_id_type=pl.DeviceIdType.MESH,
        )

    @pl.when(section == FAR)
    def _():
        for k in range(3):
            answer(2 * k + half, seq)
        for c in range(2):
            answer(2 * (FAR - 1) + c, 4 * (zbase + (x + 1) % 4) + 3)

    def near_copy(t, f, to_seq):
        return remote(
            entering.at[t, f], halo.at[t, half, f], near_send.at[f], near_recv.at[t, f],
            slot, to_seq,
        )

    def by_neighbor(t):
        return jnp.logical_or(t == 0, jnp.logical_not(jnp.logical_and(fed, half == 1)))

    def forward_copy(t, part):
        span = pl.ds(PER_PART * part, PER_PART)
        return remote(
            halo.at[t, half, span], halo.at[t, half, span], halo_send.at[1, part],
            halo_recv.at[t, 1, part], sister, seq,
        )

    def forward_wait(t, part):
        span = pl.ds(PER_PART * part, PER_PART)
        return remote(
            halo.at[t, 1 - half, span], halo.at[t, 1 - half, span], halo_send.at[1, part],
            halo_recv.at[t, 1, part], sister, seq,
        )

    def extra_copy(t, part):
        span = pl.ds(PER_PART * part, PER_PART)
        return remote(
            entering.at[t, span], halo.at[t, 2, span], halo_send.at[2, part],
            halo_recv.at[t, 2, part], sister, seq + 2 * half,
        )

    def relay_copy(t, c):
        return remote(
            relay.at[t, c], entering.at[t + 1, 2 * section + c], relay_send.at[t, c],
            back_recv.at[t + 1, 2 * section + c], 2 * FAR + half, seq,
        )

    def enter_wait(t, f):
        remote(
            entering.at[t, f], entering.at[t, f], back_send.at[0], back_recv.at[t, f], slot, seq
        ).wait_recv()

    def relay_wait(t, c):
        return remote(
            relay.at[t, c], relay.at[t, c], relay_send.at[t, c], relay_recv.at[t, c], slot, seq
        )

    def send_halo(t, part):
        @pl.when(jnp.logical_and(seq < 31, by_neighbor(t)))
        def _():
            for c in range(PER_PART):
                near_copy(t, PER_PART * part + c, seq + 1).start()

        @pl.when(gives_extra)
        def _():
            extra_copy(t, part).start()

    param_copies = [
        remote(src, dst, param_send.at[k], param_recv.at[k], sister, seq)
        for k, (src, dst) in enumerate(param_pairs)
    ]
    weight_copies = [
        remote(ref.at[0], weights.at[k, place], weight_send.at[k], weight_recv.at[k], sister, seq)
        for k, ref in enumerate(weight_refs)
    ]
    other = pl.ds(pl.multiple_of((1 - half) * 512, 512), 512)
    fresh_copy = remote(
        fresh_ref.at[:, 0, 1 - half], fresh_in, fresh_send, fresh_recv, sister, seq
    )
    for copy in param_copies:
        copy.start()
    for part in range(HALO_PARTS):
        send_halo(0, part)
    for copy in weight_copies:
        copy.start()
    fresh_copy.start()

    row_num = lax.broadcasted_iota(jnp.int32, (ROWS, ROWS), 0)
    col_num = lax.broadcasted_iota(jnp.int32, (ROWS, ROWS), 1)
    local_pairing.wait()
    for layer in range(MIXES):
        lines = pairing[layer, pl.ds(section, 1), :]
        back = jnp.where(row_num == lines, F32(1), F32(0))
        onehot[layer, 0] = back.T.astype(BF)
        onehot[layer, 1] = back.astype(BF)

    drop = jnp.full((1, ROWS), -1e30, F32)
    keep = jnp.zeros((1, ROWS), F32)
    for place_num, reach in ((0, 1 + 2 * half), (1, 2), (2, 3 - 2 * half)):
        seen = table_ref[0, half, reach - 1]
        inside = jnp.where(2 * seq + half - reach >= 0, one, zero)
        shown = jnp.full((1, ROWS), seen * inside, jnp.int32)
        earlier[:, place_num * ROWS:(place_num + 1) * ROWS] = jnp.where(shown == 1, keep, drop)
    causal = jnp.where(col_num <= row_num, F32(0), F32(-1e30))
    bias[0:ROWS] = causal
    bias[ROWS:2 * ROWS] = causal

    for copy in local_params:
        copy.wait()
    for k, (_, dst) in enumerate(
        ((None, gains.at[1 - half]), (None, angles.at[1 - half]), (None, scales.at[1 - half]))
    ):
        remote(dst, dst, param_send.at[k], param_recv.at[k], sister, seq).wait_recv()
    feature_half = mine // 4
    features = pl.ds(pl.multiple_of((mine % 4) * CHUNK, CHUNK), CHUNK)
    angle = angles[feature_half, :, 0, features]
    cosine = jnp.cos(angle)
    sine = jnp.sin(angle)
    for layer in range(MIXES):
        scale = scales[feature_half, layer, :, features]
        c = cosine[layer:layer + 1]
        n = sine[layer:layer + 1]
        coef[layer, 0:1] = scale[0:1] * c
        coef[layer, 1:2] = scale[0:1] * n
        coef[layer, 2:3] = scale[1:2] * c
        coef[layer, 3:4] = scale[1:2] * n

    def norm(block, place_num):
        total = jnp.zeros((ROWS, 1), F32)
        for f in range(CHUNKS):
            wide = block[f].astype(F32)
            total = total + jnp.sum(wide * wide, axis=-1, keepdims=True)
        factor = lax.rsqrt(total * (1.0 / WIDE) + 1e-6)
        for f in range(CHUNKS):
            part = pl.ds((f % 4) * CHUNK, CHUNK)
            gain = gains[f // 4, :, part]
            normed[place_num * ROWS:(place_num + 1) * ROWS, f * CHUNK:(f + 1) * CHUNK] = (
                block[f].astype(F32) * factor * gain
            ).astype(BF)

    def project(which, rows, target, scale=None):
        def one_part(k, carry):
            cols = pl.ds(pl.multiple_of(k * 256, 256), 256)
            product = jnp.dot(
                normed[rows, :], weights[which, :, cols], preferred_element_type=F32
            )
            if scale is None:
                target[rows, cols] = product.astype(BF)
            else:
                target[:, cols] = (product * scale).astype(BF)
            return carry

        lax.fori_loop(0, 4, one_part, 0, unroll=4)

    def await_weight(t, which):
        @pl.when(t == 0)
        def _():
            local_weights[which].wait()
            remote(
                weights.at[which, other], weights.at[which, other], weight_send.at[which],
                weight_recv.at[which], sister, seq,
            ).wait_recv()

    def mix(layer, lower, upper):
        count = len(lower)
        low = jnp.concatenate(lower, axis=1)
        up = jnp.concatenate(upper, axis=1)
        rows = [
            jnp.concatenate([coef[layer, k:k + 1]] * count, axis=1) for k in range(4)
        ]
        to_low = jnp.dot(onehot[layer, 0], up, preferred_element_type=F32)
        to_up = jnp.dot(onehot[layer, 1], low, preferred_element_type=F32)
        new_low = (rows[0] * low.astype(F32) + rows[1] * to_low).astype(BF)
        new_up = (rows[2] * up.astype(F32) - rows[3] * to_up).astype(BF)
        cut = lambda whole: [whole[:, k * CHUNK:(k + 1) * CHUNK] for k in range(count)]
        return cut(new_low), cut(new_up)

    def mix_all(layer, bit, blocks):
        lows = [b for b in range(len(blocks)) if not b >> bit & 1]
        ups = [b | 1 << bit for b in lows]
        new_low, new_up = mix(layer, [blocks[b] for b in lows], [blocks[b] for b in ups])
        result = list(blocks)
        for k, b in enumerate(lows):
            result[b] = new_low[k]
        for k, b in enumerate(ups):
            result[b] = new_up[k]
        return result

    lane = lax.broadcasted_iota(jnp.int32, (1, CHUNK), 1)
    first_head = jnp.where(lane < 64, F32(1), F32(0))
    pick_first = first_head.astype(BF)
    pick_second = (1 - first_head).astype(BF)

    def ahead_copy(t, k):
        target = (zrow + k) % 4
        c = 1
        pair = 4 * (zbase + target) + held
        return pair, remote(
            col_out.at[2 * target + c], halo.at[t + 1, c, mine], ahead_send.at[k],
            near_recv.at[t + 1, mine], 2 * section + 2 + c, jnp.minimum(pair + 1, 31),
        )

    def back_sent(t):
        @pl.when(jnp.logical_or(t == TICKS - 1, section < 7))
        def _():
            for k in range(4):
                for m in range(2):
                    target = (zrow + k) % 4
                    c = (half + m) % 2
                    sent = remote(
                        col_out.at[2 * target + c], entering.at[t + 1, mine],
                        back_send.at[2 * k + m], back_recv.at[t + 1, mine],
                        slot, seq,
                    )
                    if k or m:
                        sent.wait_send()
                    else:
                        @pl.when(jnp.logical_or(t < TICKS - 1, zrow > 0))
                        def _():
                            sent.wait_send()

        @pl.when(jnp.logical_and(feeds, t < TICKS - 1))
        def _():
            for k in range(4):
                pair, copy_ahead = ahead_copy(t, k)

                @pl.when(pair < 31)
                def _():
                    copy_ahead.wait_send()

    ones = jnp.ones((4 * ROWS, CHUNK), BF)

    def tick(t, carry):
        for step in range(HALO_PARTS):
            part = (x - zrow + step + 4) % 4

            @pl.when(jnp.logical_and(t > 0, section > 0))
            def _():
                for c in range(PER_PART):
                    enter_wait(t, PER_PART * part + c)
                send_halo(t, part)

        norm(entering.at[t], 3)
        own_rows = pl.ds(3 * ROWS, ROWS)
        await_weight(t, 0)
        project(0, own_rows, keys)
        await_weight(t, 1)
        project(1, own_rows, values)
        await_weight(t, 2)
        project(2, own_rows, queries, scale=0.125)

        @pl.when(t == 0)
        def _():
            local_fresh.wait()
            fresh_copy.wait_recv()
            for k in range(TICKS - 1):
                own = fresh_own[k].astype(F32)
                theirs = fresh_in[k].astype(F32)
                even = jnp.concatenate([own, theirs], axis=0)
                odd = jnp.concatenate([theirs, own], axis=0)
                fresh_full[k] = jnp.where(half == 0, even, odd).T.astype(BF)

                @pl.when(section == 0)
                def _():
                    entering[k + 1, 0] = fresh_full[k]

                @pl.when(section > 0)
                def _():
                    remote(
                        fresh_full.at[k], entering.at[k + 1, section], full_send.at[k],
                        back_recv.at[k + 1, section], half, seq,
                    ).start()

        for step in range(HALO_PARTS):
            part = (before % 4 - before // 4 % 4 + step + 4) % 4

            @pl.when(seq > 0)
            def _():
                for c in range(PER_PART):
                    near_copy(t, PER_PART * part + c, seq).wait_recv()
                forward_copy(t, part).start()
        for part in range(HALO_PARTS):
            @pl.when(has_extra)
            def _():
                extra_copy(t, part).wait_recv()
        norm(halo.at[t, 2], 2)
        norm(halo.at[t, half], 1)
        middle_rows = pl.ds(ROWS, 2 * ROWS)
        project(0, middle_rows, keys)
        project(1, middle_rows, values)
        for part in range(HALO_PARTS):
            @pl.when(seq > 0)
            def _():
                forward_wait(t, part).wait_recv()
        norm(halo.at[t, 1 - half], 0)
        first_rows = pl.ds(0, ROWS)
        project(0, first_rows, keys)
        project(1, first_rows, values)

        def two_heads(k, carry):
            cols = pl.ds(pl.multiple_of(k * CHUNK, CHUNK), CHUNK)
            both = queries[:, cols]
            stacked = jnp.concatenate([both * pick_first, both * pick_second], axis=0)
            scores = lax.dot_general(
                stacked, keys[:, cols], (((1,), (1,)), ((), ())), preferred_element_type=F32
            )
            scores = jnp.concatenate(
                [scores[:, :3 * ROWS] + earlier[...], scores[:, 3 * ROWS:] + bias[...]], axis=1
            )
            top = jnp.max(scores, axis=-1, keepdims=True)
            expo = jnp.exp(scores - top).astype(BF)
            with_ones = jnp.concatenate([values[:, cols], ones], axis=1)
            product = jnp.dot(expo, with_ones, preferred_element_type=F32)
            summed = product[:, :CHUNK] / product[:, CHUNK:]
            attended[:, cols] = jnp.where(lane < 64, summed[:ROWS], summed[ROWS:]).astype(BF)
            return carry

        lax.fori_loop(0, CHUNKS, two_heads, 0, unroll=8)
        await_weight(t, 3)

        @pl.when(t > 0)
        def _():
            back_sent(t - 1)

        sends = []
        for away in (2, 1, 3, 0):
            target = (x + away) % 4
            cols = pl.ds(pl.multiple_of(target * 256, 256), 256)
            product = jnp.dot(attended[...], weights[3, :, cols], preferred_element_type=F32)
            for c in range(2):
                f = 2 * target + c
                mixed[f] = (
                    entering[t, f].astype(F32) + product[:, c * CHUNK:(c + 1) * CHUNK]
                ).astype(BF)
            if away:
                for c in range(2):
                    copy = remote(
                        mixed.at[2 * target + c], row_in.at[t, mine],
                        row_send.at[2 * away - 1 + c], row_recv.at[t, mine],
                        2 * section + c, 4 * z + target,
                    )
                    copy.start()
                    sends.append(copy)
            else:
                copy = remote(
                    mixed.at[2 * x + 1 - half], row_in.at[t, mine], row_send.at[0],
                    row_recv.at[t, mine], sister, seq,
                )
                copy.start()
                sends.append(copy)
        row_in[t, mine] = mixed[mine]
        for k in range(1, CHUNKS):
            source = (mine + k) % CHUNKS
            remote(
                row_in.at[t, source], row_in.at[t, source], row_send.at[0],
                row_recv.at[t, source], slot, seq,
            ).wait_recv()
        blocks = [row_in[t, b] for b in range(CHUNKS)]
        for layer in range(3):
            blocks = mix_all(layer, layer, blocks)
        for b in range(CHUNKS):
            row_out[b] = blocks[b]

        for k in (2, 1, 3):
            target = (zrow + k) % 4
            pair = (target + x) % 4
            copy = remote(
                row_out.at[pl.ds(2 * pair, 2)], col_in.at[t, zrow], col_send.at[k - 1],
                col_recv.at[t, zrow], slot, 4 * (zbase + target) + x,
            )
            copy.start()
            sends.append(copy)
        for c in range(2):
            col_in[t, zrow, c] = row_out[2 * held + c]
        for k in range(1, 4):
            source = (zrow + k) % 4
            remote(
                col_in.at[t, source], col_in.at[t, source], col_send.at[0],
                col_recv.at[t, source], slot, seq,
            ).wait_recv()
        blocks = [col_in[t, r, c] for r in range(4) for c in range(2)]
        for layer in range(3, MIXES):
            blocks = mix_all(layer, layer - 2, blocks)
        for b in range(CHUNKS):
            col_out[b] = blocks[b]

        ahead = jnp.where(t < TICKS - 1, one, zero)
        last = t == TICKS - 1
        by_relay = jnp.logical_and(jnp.logical_and(section == FAR - 1, x < 3), t < TICKS - 1)
        direct = jnp.logical_and(
            jnp.logical_or(last, section < 7), jnp.logical_not(by_relay)
        )
        @pl.when(jnp.logical_and(crosses, t == 0))
        def _():
            pl.semaphore_wait(ready, 8)

        for k in range(4):
            target = (zrow + k) % 4
            for m in range(2):
                c = (half + m) % 2

                def back_copy():
                    return remote(
                        col_out.at[2 * target + c], entering.at[t + 1, mine],
                        back_send.at[2 * k + m], back_recv.at[t + 1, mine],
                        2 * (section + ahead) + c, 4 * (zbase + target) + held,
                    )

                if k == 0 and m == 0:
                    itself = jnp.logical_and(t == TICKS - 1, zrow == 0)

                    @pl.when(itself)
                    def _():
                        entering[t + 1, mine] = col_out[2 * target + c]

                    @pl.when(jnp.logical_and(jnp.logical_not(itself), direct))
                    def _():
                        back_copy().start()
                else:
                    @pl.when(direct)
                    def _():
                        back_copy().start()

                @pl.when(by_relay)
                def _():
                    remote(
                        col_out.at[2 * target + c], relay.at[t, half],
                        back_send.at[2 * k + m], relay_recv.at[t, half],
                        2 * x + c, 4 * (zbase + target) + held,
                    ).start()

        @pl.when(jnp.logical_and(feeds, t < TICKS - 1))
        def _():
            for k in range(4):
                pair, copy_ahead = ahead_copy(t, k)

                @pl.when(pair < 31)
                def _():
                    copy_ahead.start()

        for part in range(HALO_PARTS):
            @pl.when(jnp.logical_and(seq < 31, by_neighbor(t)))
            def _():
                for c in range(PER_PART):
                    near_copy(t, PER_PART * part + c, seq + 1).wait_send()

            @pl.when(gives_extra)
            def _():
                extra_copy(t, part).wait_send()

            @pl.when(seq > 0)
            def _():
                forward_copy(t, part).wait_send()

        @pl.when(jnp.logical_and(section == 0, t < TICKS - 1))
        def _():
            for part in range(HALO_PARTS):
                for c in range(PER_PART):
                    if part or c:
                        enter_wait(t + 1, PER_PART * part + c)
                send_halo(t + 1, part)

        @pl.when(jnp.logical_and(relays, t < TICKS - 1))
        def _():
            @pl.when(t == 0)
            def _():
                pl.semaphore_wait(ready, 1)

            for c in range(2):
                relay_wait(t, c).wait_recv()
                relay_copy(t, c).start()

        for copy in sends:
            copy.wait_send()

        @pl.when(t == 0)
        def _():
            for copy in param_copies + weight_copies + [fresh_copy]:
                copy.wait_send()

            @pl.when(section > 0)
            def _():
                for k in range(TICKS - 1):
                    remote(
                        fresh_full.at[k], entering.at[k + 1, section], full_send.at[k],
                        back_recv.at[k + 1, section], half, seq,
                    ).wait_send()

        return carry

    lax.fori_loop(0, TICKS, tick, 0)
    back_sent(TICKS - 1)

    @pl.when(relays)
    def _():
        for t in range(TICKS - 1):
            for c in range(2):
                relay_copy(t, c).wait_send()

    for f in range(CHUNKS):
        piece = remote(
            entering.at[TICKS, f], entering.at[TICKS, f], back_send.at[0],
            back_recv.at[TICKS, f], slot, seq,
        )

        @pl.when(jnp.logical_or(zrow > 0, mine != f))
        def _():
            piece.wait_recv()

        out_ref[0, 0, :, f * CHUNK:(f + 1) * CHUNK] = entering[TICKS, f]


def local(*args):
    dma = pltpu.SemaphoreType.DMA
    vmem = pl.BlockSpec(memory_space=pltpu.VMEM)
    hbm = pl.BlockSpec(memory_space=pltpu.HBM)
    smem = pl.BlockSpec(memory_space=pltpu.SMEM)
    block = (CHUNKS, ROWS, CHUNK)
    return pl.pallas_call(
        kernel,
        out_shape=jax.ShapeDtypeStruct((1, 1, ROWS, WIDE), BF),
        in_specs=[hbm] * 10 + [smem],
        out_specs=vmem,
        scratch_shapes=[
            pltpu.VMEM((4, WIDE, WIDE), BF),
            pltpu.VMEM((2, 1, 512), F32),
            pltpu.VMEM((2, MIXES, 1, 512), F32),
            pltpu.VMEM((2, MIXES, 2, 512), F32),
            pltpu.VMEM((TICKS + 1,) + block, BF),
            pltpu.VMEM((TICKS, 3) + block, BF),
            pltpu.VMEM((4 * ROWS, WIDE), BF),
            pltpu.VMEM((ROWS, WIDE), BF),
            pltpu.VMEM((4 * ROWS, WIDE), BF),
            pltpu.VMEM((4 * ROWS, WIDE), BF),
            pltpu.VMEM((ROWS, WIDE), BF),
            pltpu.VMEM(block, BF),
            pltpu.VMEM((TICKS,) + block, BF),
            pltpu.VMEM(block, BF),
            pltpu.VMEM((TICKS, 4, 2, ROWS, CHUNK), BF),
            pltpu.VMEM(block, BF),
            pltpu.VMEM((MIXES, 2, ROWS, ROWS), BF),
            pltpu.VMEM((MIXES, 4, CHUNK), F32),
            pltpu.VMEM((1, 3 * ROWS), F32),
            pltpu.VMEM((2 * ROWS, ROWS), F32),
            pltpu.VMEM((TICKS - 1, 64, ROWS), BF),
            pltpu.VMEM((TICKS - 1, 64, ROWS), BF),
            pltpu.VMEM((TICKS - 1, ROWS, CHUNK), BF),
            pltpu.VMEM((MIXES, 8, ROWS), jnp.int32),
            pltpu.VMEM((TICKS - 1, 2, ROWS, CHUNK), BF),
            pltpu.SemaphoreType.REGULAR,
            dma((CHUNKS,)), dma, dma, dma((TICKS - 1, 2)), dma((TICKS - 1, 2)),
            dma((4,)), dma((4,)), dma((4,)), dma((3,)), dma((3,)), dma((3,)),
            dma, dma, dma((TICKS - 1,)),
            dma((CHUNKS,)), dma((TICKS, CHUNKS)), dma((4,)),
            dma((3, HALO_PARTS)), dma((TICKS, 3, HALO_PARTS)),
            dma((7,)), dma((TICKS, CHUNKS)),
            dma((3,)), dma((TICKS, 4)),
            dma((CHUNKS,)), dma((TICKS + 1, CHUNKS)),
        ],
        compiler_params=pltpu.CompilerParams(
            collective_id=0, has_side_effects=True, vmem_limit_bytes=60 * 1024 * 1024
        ),
    )(*args)


def solution(mesh):
    in_specs = (
        P("seq", "section", None, None),
        P(None, "seq", None, "section", None),
        P("section", None),
        P("section", None, None),
        P("section", None, None),
        P("section", None, None),
        P("section", None, None),
        P(None, "section", None),
        P("section", None, None, None),
        P(),
        P("seq", None, None),
    )
    out_specs = P("seq", "section", None, None)

    def run(start, fresh, gain, asking, lookup, content, emitting, turning, scaling, lines, table):
        return jax.shard_map(
            local, mesh=mesh, in_specs=in_specs, out_specs=out_specs, check_vma=False
        )(
            start, jnp.swapaxes(fresh, 3, 4), gain, asking, lookup, content, emitting,
            jnp.swapaxes(turning, 0, 1), scaling, jnp.swapaxes(lines, 0, 1), table,
        )

    return run
```
